32 devices in a mesh: seq: 4 (over y, x), dp: 8 (over z, core).
Axes of the slice: x: 2, y: 2, z: 4, core: 2. Of those that a mesh axis runs over, the one named last changes fastest.
Arguments:
- tokens: bfloat16 [8, 512, 2048], P('dp', 'seq'), may hold values from -6 to 6
- segment_ids: int32 [8, 512], P('dp', 'seq'), may hold values from 0 to 511, as said below
- pad_mask: int32 [8, 512], P('dp', 'seq'), may hold values from 0 to 1, as said below
- cotangent: bfloat16 [8, 512, 2048], P('dp', 'seq'), may hold values from -6 to 6
- first_gain: bfloat16 [2048], P(('seq', 'dp')), may hold values from 0.099609375 to 1.8984375
- first_shift: bfloat16 [2048], P(('seq', 'dp')), may hold values from -1.75 to 1.75
- query_weight: bfloat16 [2048, 2048], P(('seq', 'dp')), may hold values from -0.125 to 0.125
- key_weight: bfloat16 [2048, 2048], P(('seq', 'dp')), may hold values from -0.125 to 0.125
- value_weight: bfloat16 [2048, 2048], P(('seq', 'dp')), may hold values from -0.125 to 0.125
- query_bias: bfloat16 [2048], P(('seq', 'dp')), may hold values from -1.75 to 1.75
- value_bias: bfloat16 [2048], P(('seq', 'dp')), may hold values from -1.75 to 1.75
- output_weight: bfloat16 [2048, 2048], P(('seq', 'dp')), may hold values from -1 to 1
- output_bias: bfloat16 [2048], P(('seq', 'dp')), may hold values from -1.75 to 1.75
- second_gain: bfloat16 [2048], P(('seq', 'dp')), may hold values from 0.099609375 to 1.8984375
- second_shift: bfloat16 [2048], P(('seq', 'dp')), may hold values from -1.75 to 1.75
- up_weight: bfloat16 [2048, 8192], P(('seq', 'dp')), may hold values from -0.125 to 0.125
- up_bias: bfloat16 [8192], P(('seq', 'dp')), may hold values from -1.75 to 1.75
- down_weight: bfloat16 [8192, 2048], P(('seq', 'dp')), may hold values from -0.0625 to 0.0625
- down_bias: bfloat16 [2048], P(('seq', 'dp')), may hold values from -1.75 to 1.75
Outputs:
- block_output: bfloat16 [8, 512, 2048], P('dp', 'seq')
- input_grad: float32 [8, 512, 2048], P('dp', 'seq')
- first_gain_grad: float32 [2048], P(('seq', 'dp'))
- first_shift_grad: float32 [2048], P(('seq', 'dp'))
- query_weight_grad: float32 [2048, 2048], P(('seq', 'dp'))
- key_weight_grad: float32 [2048, 2048], P(('seq', 'dp'))
- value_weight_grad: float32 [2048, 2048], P(('seq', 'dp'))
- query_bias_grad: float32 [2048], P(('seq', 'dp'))
- value_bias_grad: float32 [2048], P(('seq', 'dp'))
- output_weight_grad: float32 [2048, 2048], P(('seq', 'dp'))
- output_bias_grad: float32 [2048], P(('seq', 'dp'))
- second_gain_grad: float32 [2048], P(('seq', 'dp'))
- second_shift_grad: float32 [2048], P(('seq', 'dp'))
- up_weight_grad: float32 [2048, 8192], P(('seq', 'dp'))
- up_bias_grad: float32 [8192], P(('seq', 'dp'))
- down_weight_grad: float32 [8192, 2048], P(('seq', 'dp'))
- down_bias_grad: float32 [2048], P(('seq', 'dp'))
The draws below stay inside these ranges and needn't reach their ends.
Inputs may be any that keep to these rules, and one draw needn't show every extreme that they name: `segment_ids`: within each sequence the ids never fall; a real token's id is the position of its document's first token, and every padding token has id 512 - 1. `pad_mask`: each sequence ends in one or more padding tokens and has none elsewhere.
All inputs are finite; a program needn't handle non-finite values.
Results may differ from the reference program's by a relative error of at most 0.012.
Values may be sent and summed in bfloat16 or wider, within the bound.
No kernel may reach another device: no remote copies, remote signals or barrier semaphores. Data moves between devices by JAX's collectives and lax.ppermute only.
A program may use at most 448 MiB of HBM per device.

```python
import math
import jax
import jax.numpy as jnp
from jax import lax

D = 2048
H = 16
DH = 128
FF = 8192
TOK_DEV = 128
LENGTH = 512
SEQS = 8


def doc_layout(key):
    first_key, pad_key, end_key, mark_key, rate_key = jax.random.split(key, 5)
    position = jnp.arange(LENGTH, dtype=jnp.int32)[None, :]
    start_big = jax.random.randint(first_key, (SEQS, 1), 1, TOK_DEV)
    pad_count = jax.random.randint(pad_key, (SEQS, 1), 1, TOK_DEV // 2 + 1)
    real_end = LENGTH - pad_count
    end_big = jax.random.randint(end_key, (SEQS, 1), LENGTH - TOK_DEV + 1, real_end + 1)
    mark_rate = jax.random.randint(rate_key, (SEQS, 1), 8, 97)
    mark_draw = jax.random.randint(mark_key, (SEQS, LENGTH), 0, 1024)
    outside = (position < start_big) | (position > end_big) & (position < real_end)
    starts = (position == 0) | (position == start_big) | (position == end_big) & (end_big < real_end)
    starts = starts | outside & (mark_draw < 1024 // mark_rate)
    doc_begin = lax.cummax(jnp.where(starts, position, 0), axis=1)
    segments = jnp.where(position < real_end, doc_begin, LENGTH - 1).astype(jnp.int32)
    padding = (position < real_end).astype(jnp.int32)
    return (segments, padding)


def draw_segment_ids(key, part):
    layout = doc_layout(key)
    return layout[0]


def draw_pad_mask(key, part):
    layout = doc_layout(key)
    return layout[1]


def shard_levels(own_key, dims, cuts, least, top_value):
    def one(dim, shards_of):
        steps = jax.random.uniform(jax.random.fold_in(jax.random.fold_in(own_key, 6), dim), (shards_of,), jnp.float32, least / len(cuts), top_value / len(cuts))
        return jnp.repeat(jnp.exp(steps), dims[dim] // shards_of).reshape((-1,) + (1,) * (len(dims) - dim - 1))

    loudness = one(*cuts[0])
    for cut in cuts[1:]:
        loudness = loudness * one(*cut)
    return loudness


def bell_draw(rng, extent, width, bound, pieces=(), held_as=jnp.bfloat16):
    gain = shard_levels(rng, extent, pieces, -0.22, 0.18) if pieces else 1.0
    array = jax.random.normal(rng, extent, jnp.float32) * width * gain
    return jnp.minimum(jnp.maximum(array, -bound), bound).astype(held_as)


def setup_inputs(seed: int = 0) -> dict:
    key_of = jax.random.split(jax.random.key(seed), 20)
    tokens = bell_draw(key_of[0], (SEQS, LENGTH, D), 1.0, 6.0, ((0, 8), (1, 4)))
    segment_ids = draw_segment_ids(jax.random.fold_in(key_of[19], 71), 0)
    pad_mask = draw_pad_mask(jax.random.fold_in(key_of[19], 71), 0)
    cotangent = bell_draw(key_of[3], (SEQS, LENGTH, D), 1.0, 6.0, ((0, 8), (1, 4)))
    first_gain = jnp.clip(1.0 + 0.18 * jax.random.normal(key_of[4], (D,), jnp.float32), 0.099609375, 1.8984375).astype(jnp.bfloat16)
    first_shift = bell_draw(key_of[5], (D,), 0.3, 1.75, ((0, 32),))
    query_weight = bell_draw(key_of[6], (D, D), D ** -0.5, 0.125, ((0, 32),))
    key_weight = bell_draw(key_of[7], (D, D), D ** -0.5, 0.125, ((0, 32),))
    value_weight = bell_draw(key_of[8], (D, D), D ** -0.5, 0.125, ((0, 32),))
    query_bias = bell_draw(key_of[9], (D,), 0.3, 1.75, ((0, 32),))
    value_bias = bell_draw(key_of[10], (D,), 0.3, 1.75, ((0, 32),))
    output_weight = bell_draw(key_of[11], (D, D), (D // 64) ** -0.5, 1.0, ((0, 32),))
    output_bias = bell_draw(key_of[12], (D,), 0.3, 1.75, ((0, 32),))
    second_gain = jnp.clip(1.0 + 0.18 * jax.random.normal(key_of[13], (D,), jnp.float32), 0.099609375, 1.8984375).astype(jnp.bfloat16)
    second_shift = bell_draw(key_of[14], (D,), 0.3, 1.75, ((0, 32),))
    up_weight = bell_draw(key_of[15], (D, FF), D ** -0.5, 0.125, ((0, 32),))
    up_bias = bell_draw(key_of[16], (FF,), 0.3, 1.75, ((0, 32),))
    down_weight = bell_draw(key_of[17], (FF, D), FF ** -0.5, 0.0625, ((0, 32),))
    down_bias = bell_draw(key_of[18], (D,), 0.3, 1.75, ((0, 32),))
    return {"tokens": tokens, "segment_ids": segment_ids, "pad_mask": pad_mask, "cotangent": cotangent, "first_gain": first_gain, "first_shift": first_shift, "query_weight": query_weight, "key_weight": key_weight, "value_weight": value_weight, "query_bias": query_bias, "value_bias": value_bias, "output_weight": output_weight, "output_bias": output_bias, "second_gain": second_gain, "second_shift": second_shift, "up_weight": up_weight, "up_bias": up_bias, "down_weight": down_weight, "down_bias": down_bias}


EPSILON = 1e-05
NEGATIVE = -1e+30

@jax.custom_vjp
def low(v):
    return lax.optimization_barrier(v.astype(jnp.bfloat16)).astype(jnp.float32)

@jax.custom_vjp
def low_back(v):
    return v

def low_keep(v):
    return (low(v), None)

def low_pass(kept, grad):
    return (grad,)

def back_keep(v):
    return (v, None)

def back_low(kept, grad):
    return (low(grad),)
low.defvjp(low_keep, low_pass)
low_back.defvjp(back_keep, back_low)

def product(left_side, right_side):
    return jnp.dot(left_side, right_side, precision=lax.Precision.HIGHEST)

def layer_norm(values, gain_row, shift_row):
    center = values - lax.optimization_barrier(jnp.mean(values, axis=-1, keepdims=True))
    spread = lax.optimization_barrier(jnp.mean(center * center, axis=-1, keepdims=True))
    return center * lax.rsqrt(spread + EPSILON) * gain_row + shift_row

def head_attend(queries, keys_head, values_head, visible):
    raw_scores = low_back(product(queries, keys_head.T))
    scores = jnp.where(visible, raw_scores * (1.0 / math.sqrt(DH)), NEGATIVE)
    top_score = lax.optimization_barrier(jnp.max(scores, axis=1, keepdims=True))
    powers = jnp.exp(scores - top_score)
    weights = low(powers / lax.optimization_barrier(jnp.sum(powers, axis=1, keepdims=True)))
    return product(weights, values_head)

def forward_sequence(inputs, parameters, visible, keep_rows):
    first_gain, first_shift, query_weight, key_weight, value_weight, query_bias, value_bias, output_weight, output_bias, second_gain, second_shift, up_weight, up_bias, down_weight, down_bias = parameters
    length = inputs.shape[0]
    normed = low(layer_norm(inputs, first_gain, first_shift))
    queries = low_back(low(product(normed, query_weight) + query_bias))
    keys_all = low_back(low(product(normed, key_weight)))
    values_all = low_back(low(product(normed, value_weight) + value_bias))

    def split_heads(matrix):
        return matrix.reshape(length, H, DH).transpose(1, 0, 2)

    def per_head(members):
        return head_attend(members[0], members[1], members[2], visible)
    heads_out = lax.map(jax.checkpoint(per_head), (split_heads(queries), split_heads(keys_all), split_heads(values_all)))
    joined = low_back(low(heads_out.transpose(1, 0, 2).reshape(length, H * DH)))
    branch = low_back(product(joined, output_weight) + output_bias) * keep_rows[:, None]
    middle = inputs + branch
    second = low(layer_norm(middle, second_gain, second_shift))
    hidden = low_back(product(second, up_weight) + up_bias)
    active = low(jax.nn.gelu(hidden, approximate=False))
    return middle + product(active, down_weight) + down_bias

def reference(tokens, segment_ids, pad_mask, cotangent, first_gain, first_shift, query_weight, key_weight, value_weight, query_bias, value_bias, output_weight, output_bias, second_gain, second_shift, up_weight, up_bias, down_weight, down_bias):
    parameters = tuple((member.astype(jnp.float32) for member in (first_gain, first_shift, query_weight, key_weight, value_weight, query_bias, value_bias, output_weight, output_bias, second_gain, second_shift, up_weight, up_bias, down_weight, down_bias)))

    def one_sequence(totals, members):
        inputs, segments, padding, upstream = members
        position = jnp.arange(inputs.shape[0], dtype=jnp.int32)
        same_doc = (segments[None, :] == segments[:, None]) & (padding[None, :] == 1)
        visible = (position[None, :] <= position[:, None]) & (same_doc | (position[None, :] == position[:, None]))
        keep_rows = padding.astype(jnp.float32)
        result, pullback = jax.vjp(lambda source, weights: forward_sequence(source, weights, visible, keep_rows), inputs, parameters)
        input_grad, weight_grads = pullback(upstream)
        totals = jax.tree.map(lambda running, addend: running + addend, totals, weight_grads)
        return (totals, (result, input_grad))
    initial = jax.tree.map(jnp.zeros_like, parameters)
    totals, (results, input_grads) = lax.scan(one_sequence, initial, (tokens.astype(jnp.float32), segment_ids, pad_mask, cotangent.astype(jnp.float32)))
    return (results.astype(jnp.bfloat16), input_grads, totals[0], totals[1], totals[2], totals[3], totals[4], totals[5], totals[6], totals[7], totals[8], totals[9], totals[10], totals[11], totals[12], totals[13], totals[14])
```

```python
import math

import jax
import jax.numpy as jnp
from jax import lax
from jax.sharding import Mesh
from jax.sharding import PartitionSpec as P

H = 16
DH = 128
EPSILON = 1e-05
NEGATIVE = -1e30
BF = jnp.bfloat16
F32 = jnp.float32


def dot(form, left, right):
    return jnp.einsum(form, left, right, preferred_element_type=F32)


def normalize(v):
    center = v - jnp.mean(v, axis=-1, keepdims=True)
    inv = lax.rsqrt(jnp.mean(center * center, axis=-1, keepdims=True) + EPSILON)
    return center * inv, inv


def norm_back(xhat, inv, e):
    return (
        e - jnp.mean(e, axis=-1, keepdims=True) - xhat * jnp.mean(e * xhat, axis=-1, keepdims=True)
    ) * inv


def make_body(S, Z):
    bits = [1 << b for b in range(S.bit_length() - 1)]
    halves = len(bits) if len(bits) > 1 else 1

    def xor_seq(v, q):
        return lax.ppermute(v, "seq", [(i, i ^ q) for i in range(S)])

    def swap_core(v):
        return lax.ppermute(v, "core", [(0, 1), (1, 0)])

    def rotation(h):
        return bits[h:] + bits[:h] if bits else []

    def plane_gather(v):
        pieces = jnp.split(v, 2, axis=0)
        done = []
        for h, piece in enumerate(pieces):
            held = {0: piece}
            for b in rotation(h):
                order = sorted(held)
                got = xor_seq(jnp.concatenate([held[q] for q in order], axis=0), b)
                got = jnp.split(got, len(order), axis=0)
                for q, g in zip(order, got):
                    held[q ^ b] = g
            done.append([held[q] for q in range(S)])
        own = jnp.concatenate([done[h][q] for h in range(2) for q in range(S)], axis=0)
        other = swap_core(own)
        return jnp.concatenate([own, other], axis=0)

    def plane_scatter(v):
        rows, feat = v.shape
        t = rows // (2 * S)
        mine, theirs = v[: rows // 2], v[rows // 2 :].astype(BF)
        total = mine + swap_core(theirs).astype(F32)
        total = total.reshape(2, S, t // 2, feat)
        out = []
        for h in range(2):
            held = {q: total[h, q] for q in range(S)}
            for b in reversed(rotation(h)):
                order = sorted(q for q in held if q & b)
                sent = jnp.concatenate([held[q].astype(BF) for q in order], axis=0)
                got = jnp.split(xor_seq(sent, b), len(order), axis=0)
                kept = {}
                for q, g in zip(order, got):
                    kept[q ^ b] = held[q ^ b] + g.astype(F32)
                held = kept
            out.append(held[0])
        return jnp.concatenate(out, axis=0)

    def line_gather(v):
        z = lax.axis_index("z")
        up, down = [v], [v]
        for k in range(1, Z):
            up.append(lax.ppermute(up[-1], "z", [(i, i + 1) for i in range(k - 1, Z - 1)]))
            down.append(lax.ppermute(down[-1], "z", [(i, i - 1) for i in range(1, Z - k + 1)]))
        return [v] + [jnp.where(z + m < Z, down[m], up[Z - m]) for m in range(1, Z)]

    def line_scatter(pieces):
        up = down = None
        for k in range(1, Z):
            a = pieces[Z - k] if up is None else (pieces[Z - k].astype(F32) + up.astype(F32)).astype(BF)
            b = pieces[k] if down is None else (pieces[k].astype(F32) + down.astype(F32)).astype(BF)
            up = lax.ppermute(a, "z", [(i, i + 1) for i in range(k)])
            down = lax.ppermute(b, "z", [(i, i - 1) for i in range(Z - k, Z)])
        total = pieces[0].astype(F32)
        if Z > 1:
            total = total + up.astype(F32) + down.astype(F32)
        return total

    def roll(v, axis, back=False):
        z = lax.axis_index("z")
        start = (Z - z) % Z if back else z
        return lax.dynamic_slice_in_dim(jnp.concatenate([v, v], axis=axis), start, Z, axis=axis)

    def to_relative(v):
        rows, feat = v.shape
        v = v.reshape(rows, S, Z, feat // (S * Z)).transpose(0, 2, 1, 3)
        return roll(v, 1).reshape(rows, feat)

    def from_relative(v):
        rows, feat = v.shape
        v = roll(v.reshape(rows, Z, S, feat // (S * Z)), 1, back=True)
        return v.transpose(0, 2, 1, 3).reshape(rows, feat)

    def roll_columns(v, back=False):
        rows, feat = v.shape
        return roll(v.reshape(rows, Z, feat // Z), 1, back).reshape(rows, feat)

    def exchange(v):
        return lax.all_to_all(v, ("seq", "core"), split_axis=0, concat_axis=0, tiled=True)

    def body(
        tokens, segment_ids, pad_mask, cotangent,
        first_gain, first_shift, query_weight, key_weight, value_weight, query_bias, value_bias,
        output_weight, output_bias, second_gain, second_shift, up_weight, up_bias, down_weight, down_bias,
    ):
        s, z, c = lax.axis_index("seq"), lax.axis_index("z"), lax.axis_index("core")
        n = S * Z * 2
        R, D = query_weight.shape
        RF = down_weight.shape[0]
        t = tokens.shape[1]
        L = S * t
        heads_own = H // (2 * S)
        cols = D // (2 * S)
        scale = 1.0 / math.sqrt(DH)

        small = jnp.concatenate(
            [first_gain, first_shift, query_bias, value_bias, output_bias, second_gain, second_shift, down_bias, up_bias]
        )[None]
        small = jnp.concatenate([small, swap_core(small)], axis=0)
        small = jnp.concatenate([small] + [xor_seq(small, q) for q in range(1, S)], axis=0)
        small = jnp.concatenate(
            [small] + [lax.ppermute(small, "z", [(i, (i - m) % Z) for i in range(Z)]) for m in range(1, Z)], axis=0
        )
        slot = jnp.arange(n)
        place = ((s ^ (slot // 2 % S)) * Z + (z + slot // (2 * S)) % Z) * 2 + (c ^ (slot % 2))
        order = (place[None, :] == slot[:, None]).astype(BF)
        small = dot("ab,bf->af", order, small)
        fields = [small[:, i * R : (i + 1) * R].reshape(-1) for i in range(8)]
        g1, b1, qb, vb, ob, g2, b2, db = fields
        ub = small[:, 8 * R :].reshape(S, Z, 2, RF)

        codes = jnp.stack([segment_ids[0], pad_mask[0]])
        codes = jnp.stack([codes] + [xor_seq(codes, q) for q in range(1, S)])
        codes = jnp.stack([codes, swap_core(codes)])
        codes = codes.reshape(2, S, 2, 2, t // 2).transpose(2, 0, 3, 1, 4).reshape(2, 2, L)
        segments, padding = codes[0], codes[1]
        where_q = (s ^ jnp.arange(S)) * t
        position = (
            where_q[None, :, None] + jnp.arange(2)[:, None, None] * (t // 2) + jnp.arange(t // 2)[None, None, :]
        ).reshape(L)
        same = (segments[:, None, :] == segments[:, :, None]) & (padding[:, None, :] == 1)
        later = position[None, :] <= position[:, None]
        itself = position[None, :] == position[:, None]
        visible = (later[None] & (same | itself[None]))[:, None]
        keep = pad_mask[0].astype(F32)[:, None]

        wo_pieces = line_gather(output_weight)
        qkv = jnp.stack([query_weight, key_weight, value_weight], axis=1).reshape(R, 3, S * 2, cols)
        qkv = exchange(qkv.transpose(2, 0, 1, 3)).reshape(S * 2 * R, 3 * cols)
        wqkv = jnp.concatenate(line_gather(qkv), axis=0)
        up = up_weight.reshape(R, S, Z, 2, RF).transpose(1, 3, 0, 2, 4).reshape(S * 2, R, Z * RF)
        up = exchange(up).reshape(S * 2 * R, Z * RF)
        wup = jnp.concatenate(line_gather(up), axis=0)
        wdown = jnp.concatenate(line_gather(down_weight), axis=0)

        half = Z // 2
        wo = roll(jnp.stack(wo_pieces), 0, back=True)
        keep_part = lax.dynamic_slice_in_dim(wo, c * half, half, axis=0)
        send_part = lax.dynamic_slice_in_dim(wo, (1 - c) * half, half, axis=0)
        got_part = swap_core(send_part)
        wo = jnp.where(
            c == 0,
            jnp.stack([keep_part, got_part], axis=1),
            jnp.stack([got_part, keep_part], axis=1),
        ).reshape(cols, D)

        xf = tokens[0].astype(F32)
        dy = cotangent[0]
        dyf = dy.astype(F32)
        xhat1, inv1 = normalize(xf)
        normed = plane_gather(to_relative((xhat1 * g1 + b1).astype(BF)))
        dy_all = plane_gather(dy)
        qkv_bias = jnp.stack([qb.reshape(S * 2, cols), jnp.zeros((S * 2, cols), F32), vb.reshape(S * 2, cols)], axis=1)
        qkv_bias = lax.dynamic_index_in_dim(qkv_bias, s * 2 + c, 0, keepdims=False).reshape(3 * cols)
        qkv_out = (dot("td,de->te", normed, wqkv) + qkv_bias).astype(BF)
        split = qkv_out.reshape(2, L, 3, heads_own, DH).transpose(2, 0, 3, 1, 4)
        q, k, v = split[0], split[1], split[2]
        scores = jnp.where(visible, dot("bhqd,bhkd->bhqk", q, k) * scale, NEGATIVE)
        top = jnp.max(scores, axis=-1, keepdims=True)
        powers = jnp.exp(scores - top)
        sums = jnp.sum(powers, axis=-1, keepdims=True)
        probs = powers / sums
        out = dot("bhqk,bhkd->bqhd", probs.astype(BF), v)
        heads = out.astype(BF).reshape(2 * L, cols)
        branch = plane_scatter(dot("td,de->te", heads, wo))
        middle = xf + (branch + ob) * keep
        xhat2, inv2 = normalize(middle)
        second = plane_gather(to_relative((xhat2 * g2 + b2).astype(BF)))
        up_row = lax.dynamic_index_in_dim(lax.dynamic_index_in_dim(ub, s, 0, False), c, 1, False).reshape(Z * RF)
        hidden = dot("td,df->tf", second, wup) + up_row
        phi = 0.5 * (1.0 + lax.erf(hidden * math.sqrt(0.5)))
        slope = phi + hidden * jnp.exp(-0.5 * hidden * hidden) * (1.0 / math.sqrt(2 * math.pi))
        active = roll_columns((hidden * phi).astype(BF))

        dactive = roll_columns(dot("td,fd->tf", dy_all, wdown), back=True)
        dhidden = (dactive * slope).astype(BF)
        down_pieces = jnp.split(dot("tf,td->fd", active, dy_all).astype(BF), Z, axis=0)
        down_weight_grad = line_scatter(down_pieces)
        dsecond = from_relative(plane_scatter(dot("tf,df->td", dhidden, wup)))
        up_pieces = jnp.split(dot("td,tf->df", second, dhidden).astype(BF), Z, axis=0)
        up_grad = line_scatter(up_pieces)
        result = plane_scatter(dot("tf,fd->td", active, wdown))
        block_output = (middle + result + db).astype(BF)
        e2 = g2 * dsecond
        dmiddle = dyf + norm_back(xhat2, inv2, e2)
        dbranch = (dmiddle * keep).astype(BF)
        dbranch_all = plane_gather(dbranch)
        dheads = dot("te,de->td", dbranch_all, wo).astype(BF)
        wo_grad = dot("td,te->de", heads, dbranch_all).astype(BF).reshape(half, 2, R, D)
        keep_part = lax.dynamic_index_in_dim(wo_grad, c, 1, False)
        got_part = swap_core(lax.dynamic_index_in_dim(wo_grad, 1 - c, 1, False))
        wo_grad = jnp.where(
            c == 0,
            jnp.concatenate([keep_part, got_part], axis=0),
            jnp.concatenate([got_part, keep_part], axis=0),
        )
        wo_grad = roll(wo_grad, 0)
        output_weight_grad = line_scatter([wo_grad[m] for m in range(Z)])
        dh = dheads.reshape(2, L, heads_own, DH).transpose(0, 2, 1, 3)
        dp = dot("bhqd,bhkd->bhqk", dh, v)
        delta = jnp.sum(probs * dp, axis=-1, keepdims=True)
        dscores = (probs * (dp - delta) * scale).astype(BF)
        dq = dot("bhqk,bhkd->bqhd", dscores, k)
        dk = dot("bhqk,bhqd->bkhd", dscores, q)
        dv = dot("bhqk,bhqd->bkhd", probs.astype(BF), dh)
        dqkv = jnp.stack([dq, dk, dv], axis=2).astype(BF).reshape(2 * L, 3 * cols)
        qkv_pieces = jnp.split(dot("td,te->de", normed, dqkv).astype(BF), Z, axis=0)
        qkv_grad = line_scatter(qkv_pieces)
        dnormed = from_relative(plane_scatter(dot("te,de->td", dqkv, wqkv)))
        input_grad = dmiddle + norm_back(xhat1, inv1, g1 * dnormed)

        qkv_grad = exchange(qkv_grad.astype(BF).reshape(S * 2, R, 3 * cols))
        qkv_grad = qkv_grad.reshape(S * 2, R, 3, cols).transpose(2, 1, 0, 3).reshape(3, R, D).astype(F32)
        up_grad = exchange(up_grad.astype(BF).reshape(S * 2, R, Z * RF))
        up_weight_grad = up_grad.reshape(S, 2, R, Z, RF).transpose(2, 0, 3, 1, 4).reshape(R, -1).astype(F32)

        bias = jnp.sum(dqkv.astype(F32), axis=0).reshape(3, cols)
        spread = jnp.zeros((2, S * 2, cols), F32)
        spread = lax.dynamic_update_slice(spread, jnp.stack([bias[0], bias[2]])[:, None], (0, s * 2 + c, 0))
        wide = jnp.zeros((S, Z, 2, RF), F32)
        wide = lax.dynamic_update_slice(
            wide, jnp.sum(dhidden.astype(F32), axis=0).reshape(1, Z, 1, RF), (s, 0, c, 0)
        )
        rows = [
            jnp.sum(dnormed * xhat1, axis=0),
            jnp.sum(dnormed, axis=0),
            spread[0].reshape(-1),
            spread[1].reshape(-1),
            jnp.sum(dbranch.astype(F32), axis=0),
            jnp.sum(dsecond * xhat2, axis=0),
            jnp.sum(dsecond, axis=0),
            jnp.sum(dyf, axis=0),
        ]
        packed = jnp.concatenate([r.reshape(n, R) for r in rows] + [wide.reshape(n, RF)], axis=1)
        packed = lax.psum_scatter(packed, ("seq", "z", "core"), scatter_dimension=0, tiled=True)[0]
        sg = [packed[i * R : (i + 1) * R] for i in range(8)]
        return (
            block_output[None],
            input_grad[None],
            sg[0],
            sg[1],
            qkv_grad[0],
            qkv_grad[1],
            qkv_grad[2],
            sg[2],
            sg[3],
            output_weight_grad,
            sg[4],
            sg[5],
            sg[6],
            up_weight_grad,
            packed[8 * R :],
            down_weight_grad,
            sg[7],
        )

    return body


def solution(mesh):
    S, DP = mesh.shape["seq"], mesh.shape["dp"]
    Z = DP // 2
    parts = Mesh(mesh.devices.reshape(S, Z, 2), ("seq", "z", "core"))
    every = ("seq", "z", "core")
    token = P(("z", "core"), "seq", None)
    code = P(("z", "core"), "seq")
    vector = P(every)
    matrix = P(every, None)
    return jax.shard_map(
        make_body(S, Z),
        mesh=parts,
        in_specs=(
            token, code, code, token,
            vector, vector, matrix, matrix, matrix, vector, vector,
            matrix, vector, vector, vector, matrix, vector, matrix, vector,
        ),
        out_specs=(
            token, token, vector, vector, matrix, matrix, matrix, vector, vector,
            matrix, vector, vector, vector, matrix, vector, matrix, vector,
        ),
        check_vma=False,
    )
```

```python
import functools
import math

import jax
import jax.numpy as jnp
from jax import lax
from jax.experimental import pallas as pl
from jax.experimental.pallas import tpu as pltpu
from jax.sharding import Mesh
from jax.sharding import PartitionSpec as P

H = 16
DH = 128
EPSILON = 1e-05
NEGATIVE = -1e30
BF = jnp.bfloat16
F32 = jnp.float32
SCALE = 1.0 / math.sqrt(DH)


def dot(form, left, right):
    return jnp.einsum(form, left, right, preferred_element_type=F32)


def normalize(v):
    center = v - jnp.mean(v, axis=-1, keepdims=True)
    inv = lax.rsqrt(jnp.mean(center * center, axis=-1, keepdims=True) + EPSILON)
    return center * inv, inv


def norm_back(xhat, inv, e):
    return (
        e - jnp.mean(e, axis=-1, keepdims=True) - xhat * jnp.mean(e * xhat, axis=-1, keepdims=True)
    ) * inv


def nt(a, b):
    return lax.dot_general(a, b, (((1,), (1,)), ((), ())), preferred_element_type=F32)


def nn(a, b):
    return lax.dot_general(a, b, (((1,), (0,)), ((), ())), preferred_element_type=F32)


def tn(a, b):
    return lax.dot_general(a, b, (((0,), (0,)), ((), ())), preferred_element_type=F32)


def seen(q_ref, k_ref):
    q_pos, q_doc = q_ref[:, 0:1], q_ref[:, 1:2]
    k_pos, k_doc = k_ref[0:1, :], k_ref[1:2, :]
    return ((k_pos <= q_pos) & (k_doc == q_doc)) | (k_pos == q_pos)


def softmax(q, k, visible):
    scores = jnp.where(visible, nt(q, k) * SCALE, NEGATIVE)
    powers = jnp.exp(scores - jnp.max(scores, axis=1, keepdims=True))
    return powers / jnp.sum(powers, axis=1, keepdims=True)


def attend_kernel(heads, q_info, k_info, qkv_ref, out_ref):
    visible = seen(q_info, k_info)
    for h in range(heads):
        q, k, v = (qkv_ref[:, (part * heads + h) * DH : (part * heads + h + 1) * DH] for part in range(3))
        probs = softmax(q, k, visible).astype(BF)
        out_ref[:, h * DH : (h + 1) * DH] = nn(probs, v).astype(BF)


def attend_back_kernel(heads, q_info, k_info, qkv_ref, grad_ref, out_ref):
    visible = seen(q_info, k_info)
    for h in range(heads):
        q, k, v = (qkv_ref[:, (part * heads + h) * DH : (part * heads + h + 1) * DH] for part in range(3))
        grad = grad_ref[:, h * DH : (h + 1) * DH]
        probs = softmax(q, k, visible)
        dp = nt(grad, v)
        delta = jnp.sum(probs * dp, axis=1, keepdims=True)
        dscores = (probs * (dp - delta) * SCALE).astype(BF)
        parts = (nn(dscores, k), tn(dscores, q), tn(probs.astype(BF), grad))
        for part, value in enumerate(parts):
            out_ref[:, (part * heads + h) * DH : (part * heads + h + 1) * DH] = value.astype(BF)


def attend_call(kernel, heads, columns, matmuls, *args):
    rows = args[2].shape[0]
    return pl.pallas_call(
        functools.partial(kernel, heads),
        out_shape=jax.ShapeDtypeStruct((rows, columns), BF),
        compiler_params=pltpu.CompilerParams(vmem_limit_bytes=56 * 1024 * 1024),
        cost_estimate=pl.CostEstimate(
            flops=2 * matmuls * heads * rows * rows * DH, bytes_accessed=8 * rows * columns, transcendentals=heads * rows * rows
        ),
    )(*args)


def make_body(S, Z):
    def xor_seq(v, q):
        return lax.ppermute(v, "seq", [(i, i ^ q) for i in range(S)])

    def swap_core(v):
        return lax.ppermute(v, "core", [(0, 1), (1, 0)])

    def plane_gather(v):
        own = jnp.concatenate([v] + [xor_seq(v, q) for q in range(1, S)], axis=0)
        return own, swap_core(own)

    def plane_scatter(make):
        got = swap_core(make(1).astype(BF))
        total = make(0) + got.astype(F32)
        blocks = total.reshape(S, -1, total.shape[1])
        mine = blocks[0]
        for q in range(1, S):
            mine = mine + xor_seq(blocks[q].astype(BF), q).astype(F32)
        return mine

    def everyone(v):
        return lax.all_to_all(v, ("seq", "z", "core"), split_axis=0, concat_axis=0, tiled=True)

    def in_plane(v):
        return lax.all_to_all(v, ("seq", "core"), split_axis=0, concat_axis=0, tiled=True)

    def body(
        tokens, segment_ids, pad_mask, cotangent,
        first_gain, first_shift, query_weight, key_weight, value_weight, query_bias, value_bias,
        output_weight, output_bias, second_gain, second_shift, up_weight, up_bias, down_weight, down_bias,
    ):
        s, z, c = lax.axis_index("seq"), lax.axis_index("z"), lax.axis_index("core")
        n, tp = S * Z * 2, S * 2
        R, D = query_weight.shape
        RF = down_weight.shape[0]
        t = tokens.shape[1]
        L = S * t
        heads_own = H // tp
        cols = D // tp
        half = Z // 2

        def to_weight_order(v):
            return v.reshape(-1, S, Z, 2 * R).transpose(0, 2, 1, 3).reshape(-1, D)

        def from_weight_order(v):
            return v.reshape(-1, Z, S, 2 * R).transpose(0, 2, 1, 3).reshape(-1, D)

        qkv = jnp.stack([query_weight, key_weight, value_weight], axis=1).reshape(R, 3, tp, cols)
        qkv = qkv.transpose(2, 0, 1, 3).reshape(S, 1, 2, R, 3 * cols)
        qkv = jnp.broadcast_to(qkv, (S, Z, 2, R, 3 * cols)).reshape(n, R, 3 * cols)
        wqkv = everyone(qkv).reshape(D, 3 * cols)
        rows_of = lax.all_gather(jnp.concatenate([output_weight, down_weight], axis=0), "z", axis=0)
        wdown = rows_of[:, R:].reshape(Z * RF, D)
        wo = rows_of[:, :R]
        keep_part = lax.dynamic_slice_in_dim(wo, c * half, half, axis=0)
        got_part = swap_core(lax.dynamic_slice_in_dim(wo, (1 - c) * half, half, axis=0))
        wo = jnp.where(
            c == 0,
            jnp.stack([keep_part, got_part], axis=1),
            jnp.stack([got_part, keep_part], axis=1),
        ).reshape(cols, D)
        up = up_weight.reshape(R, S, Z, 2, RF).transpose(1, 3, 0, 2, 4).reshape(tp, R, Z * RF)
        wup = lax.all_gather(in_plane(up).reshape(tp * R, Z * RF), "z", axis=0, tiled=True)

        small = jnp.concatenate(
            [first_gain, first_shift, query_bias, value_bias, output_bias, second_gain, second_shift, down_bias, up_bias]
        )
        small = everyone(jnp.broadcast_to(small[None], (n, small.shape[0]))).astype(F32)
        g1, b1, qb, vb, ob, g2, b2, db = [small[:, i * R : (i + 1) * R].reshape(-1) for i in range(8)]
        ub = small[:, 8 * R :].reshape(S, Z, 2, RF)

        codes = jnp.stack([segment_ids[0], pad_mask[0]])
        codes = jnp.stack([codes] + [xor_seq(codes, q) for q in range(1, S)], axis=1)
        codes = [codes.reshape(2, L), swap_core(codes).reshape(2, L)]
        position = ((s ^ jnp.arange(S, dtype=jnp.int32))[:, None] * t + jnp.arange(t, dtype=jnp.int32)[None]).reshape(L)
        q_info = [jnp.stack([position, code[0]], axis=1) for code in codes]
        k_info = [jnp.stack([position, jnp.where(code[1] == 1, code[0], -1)]) for code in codes]
        keep = pad_mask[0].astype(F32)[:, None]

        xf = tokens[0].astype(F32)
        dy = cotangent[0]
        dyf = dy.astype(F32)
        xhat1, inv1 = normalize(xf)
        normed = plane_gather((xhat1 * g1 + b1).astype(BF))
        dy_all = plane_gather(dy)
        qkv_bias = jnp.stack([qb.reshape(tp, cols), jnp.zeros((tp, cols), F32), vb.reshape(tp, cols)], axis=1)
        qkv_bias = lax.dynamic_index_in_dim(qkv_bias, s * 2 + c, 0, keepdims=False).reshape(3 * cols)
        both = range(2)
        qkv_out = [(dot("td,de->te", normed[e], wqkv) + qkv_bias).astype(BF) for e in both]
        heads = [
            attend_call(attend_kernel, heads_own, cols, 2, q_info[e], k_info[e], qkv_out[e]) for e in both
        ]
        branch = plane_scatter(lambda e: dot("td,de->te", heads[e], wo))
        middle = xf + (branch + ob) * keep
        xhat2, inv2 = normalize(middle)
        second = plane_gather(to_weight_order((xhat2 * g2 + b2).astype(BF)))
        up_row = lax.dynamic_index_in_dim(lax.dynamic_index_in_dim(ub, s, 0, False), c, 1, False).reshape(Z * RF)
        active, dhidden = [], []
        for e in both:
            hidden = dot("td,df->tf", second[e], wup) + up_row
            phi = 0.5 * (1.0 + lax.erf(hidden * math.sqrt(0.5)))
            slope = phi + hidden * jnp.exp(-0.5 * hidden * hidden) * (1.0 / math.sqrt(2 * math.pi))
            active.append((hidden * phi).astype(BF))
            dhidden.append((dot("td,fd->tf", dy_all[e], wdown) * slope).astype(BF))

        dsecond = from_weight_order(plane_scatter(lambda e: dot("tf,df->td", dhidden[e], wup)))
        join = functools.partial(jnp.concatenate, axis=0)
        dy_join, active_join, second_join, dhidden_join = join(dy_all), join(active), join(second), join(dhidden)
        down_grad = dot("tf,td->fd", active_join, dy_join).astype(BF)
        down_weight_grad = lax.psum_scatter(down_grad, "z", scatter_dimension=0, tiled=True).astype(F32)
        up_grad = dot("td,tf->df", second_join, dhidden_join).astype(BF)
        up_grad = lax.psum_scatter(up_grad, "z", scatter_dimension=0, tiled=True)
        up_grad = in_plane(up_grad.reshape(tp, R, Z * RF))
        up_weight_grad = up_grad.reshape(S, 2, R, Z, RF).transpose(2, 0, 3, 1, 4).reshape(R, -1).astype(F32)
        result = plane_scatter(lambda e: dot("tf,fd->td", active[e], wdown))
        block_output = (middle + result + db).astype(BF)
        dmiddle = dyf + norm_back(xhat2, inv2, g2 * dsecond)
        dbranch = (dmiddle * keep).astype(BF)
        dbranch_all = plane_gather(dbranch)
        dheads = [dot("te,de->td", dbranch_all[e], wo).astype(BF) for e in both]
        wo_grad = dot("td,te->de", join(heads), join(dbranch_all)).astype(BF).reshape(half, 2, R, D)
        keep_part = lax.dynamic_index_in_dim(wo_grad, c, 1, False)
        got_part = swap_core(lax.dynamic_index_in_dim(wo_grad, 1 - c, 1, False))
        wo_grad = jnp.where(c == 0, join([keep_part, got_part]), join([got_part, keep_part]))
        output_weight_grad = lax.psum_scatter(wo_grad, "z", scatter_dimension=0, tiled=True)[0].astype(F32)
        dqkv = [
            attend_call(attend_back_kernel, heads_own, 3 * cols, 5, q_info[e], k_info[e], qkv_out[e], dheads[e]) for e in both
        ]
        dqkv_join = join(dqkv)
        qkv_grad = dot("td,te->de", join(normed), dqkv_join).astype(BF).reshape(n, R, 3 * cols)
        qkv_grad = everyone(qkv_grad).reshape(S, Z, 2, R, 3, cols)
        qkv_grad = jnp.sum(qkv_grad.astype(F32), axis=1).transpose(3, 2, 0, 1, 4).reshape(3, R, D)
        dnormed = plane_scatter(lambda e: dot("te,de->td", dqkv[e], wqkv))
        input_grad = dmiddle + norm_back(xhat1, inv1, g1 * dnormed)

        bias = jnp.sum(dqkv_join.astype(F32), axis=0).reshape(3, cols)
        spread = jnp.zeros((2, tp, cols), F32)
        spread = lax.dynamic_update_slice(spread, jnp.stack([bias[0], bias[2]])[:, None], (0, s * 2 + c, 0))
        wide = jnp.zeros((S, Z, 2, RF), F32)
        wide = lax.dynamic_update_slice(
            wide, jnp.sum(dhidden_join.astype(F32), axis=0).reshape(1, Z, 1, RF), (s, 0, c, 0)
        )

        def share(vectors):
            packed = jnp.concatenate([v.reshape(n, -1) for v in vectors], axis=1)
            packed = jnp.sum(everyone(packed), axis=0)
            out, at = [], 0
            for v in vectors:
                out.append(packed[at : at + v.size // n])
                at += v.size // n
            return out

        ob_grad, g2_grad, b2_grad, db_grad, ub_grad, qb_grad, vb_grad = share(
            [
                jnp.sum(dbranch.astype(F32), axis=0),
                jnp.sum(dsecond * xhat2, axis=0),
                jnp.sum(dsecond, axis=0),
                jnp.sum(dyf, axis=0),
                wide,
                spread[0],
                spread[1],
            ]
        )
        g1_grad, b1_grad = share([jnp.sum(dnormed * xhat1, axis=0), jnp.sum(dnormed, axis=0)])
        return (
            block_output[None], input_grad[None], g1_grad, b1_grad,
            qkv_grad[0], qkv_grad[1], qkv_grad[2], qb_grad, vb_grad,
            output_weight_grad, ob_grad, g2_grad, b2_grad,
            up_weight_grad, ub_grad, down_weight_grad, db_grad,
        )

    return body


def solution(mesh):
    S, DP = mesh.shape["seq"], mesh.shape["dp"]
    Z = DP // 2
    parts = Mesh(mesh.devices.reshape(S, Z, 2), ("seq", "z", "core"))
    every = ("seq", "z", "core")
    token = P(("z", "core"), "seq", None)
    code = P(("z", "core"), "seq")
    vector = P(every)
    matrix = P(every, None)
    return jax.shard_map(
        make_body(S, Z),
        mesh=parts,
        in_specs=(
            token, code, code, token,
            vector, vector, matrix, matrix, matrix, vector, vector,
            matrix, vector, vector, vector, matrix, vector, matrix, vector,
        ),
        out_specs=(
            token, token, vector, vector, matrix, matrix, matrix, vector, vector,
            matrix, vector, vector, vector, matrix, vector, matrix, vector,
        ),
        check_vma=False,
    )
```

```python
import functools
import math

import jax
import jax.numpy as jnp
from jax import lax
from jax.experimental import pallas as pl
from jax.experimental.pallas import tpu as pltpu
from jax.sharding import Mesh
from jax.sharding import PartitionSpec as P

H = 16
DH = 128
EPSILON = 1e-05
NEGATIVE = -1e30
BF = jnp.bfloat16
F32 = jnp.float32
SCALE = 1.0 / math.sqrt(DH)


def dot(form, left, right):
    return jnp.einsum(form, left, right, preferred_element_type=F32)


def normalize(v):
    center = v - jnp.mean(v, axis=-1, keepdims=True)
    inv = lax.rsqrt(jnp.mean(center * center, axis=-1, keepdims=True) + EPSILON)
    return center * inv, inv


def norm_back(xhat, inv, e):
    return (
        e - jnp.mean(e, axis=-1, keepdims=True) - xhat * jnp.mean(e * xhat, axis=-1, keepdims=True)
    ) * inv


def nt(a, b):
    return lax.dot_general(a, b, (((1,), (1,)), ((), ())), preferred_element_type=F32)


def nn(a, b):
    return lax.dot_general(a, b, (((1,), (0,)), ((), ())), preferred_element_type=F32)


def tn(a, b):
    return lax.dot_general(a, b, (((0,), (0,)), ((), ())), preferred_element_type=F32)


def seen(q_ref, k_ref):
    q_pos, q_doc = q_ref[:, 0:1], q_ref[:, 1:2]
    k_pos, k_doc = k_ref[0:1, :], k_ref[1:2, :]
    return ((k_pos <= q_pos) & (k_doc == q_doc)) | (k_pos == q_pos)


def softmax(q, k, visible):
    scores = jnp.where(visible, nt(q, k) * SCALE, NEGATIVE)
    powers = jnp.exp(scores - jnp.max(scores, axis=1, keepdims=True))
    return powers / jnp.sum(powers, axis=1, keepdims=True)


def attend_kernel(heads, q_info, k_info, qkv_ref, out_ref):
    visible = seen(q_info, k_info)
    for h in range(heads):
        q, k, v = (qkv_ref[:, (part * heads + h) * DH : (part * heads + h + 1) * DH] for part in range(3))
        probs = softmax(q, k, visible).astype(BF)
        out_ref[:, h * DH : (h + 1) * DH] = nn(probs, v).astype(BF)


def attend_back_kernel(heads, q_info, k_info, qkv_ref, grad_ref, out_ref):
    visible = seen(q_info, k_info)
    for h in range(heads):
        q, k, v = (qkv_ref[:, (part * heads + h) * DH : (part * heads + h + 1) * DH] for part in range(3))
        grad = grad_ref[:, h * DH : (h + 1) * DH]
        probs = softmax(q, k, visible)
        dp = nt(grad, v)
        delta = jnp.sum(probs * dp, axis=1, keepdims=True)
        dscores = (probs * (dp - delta) * SCALE).astype(BF)
        parts = (nn(dscores, k), tn(dscores, q), tn(probs.astype(BF), grad))
        for part, value in enumerate(parts):
            out_ref[:, (part * heads + h) * DH : (part * heads + h + 1) * DH] = value.astype(BF)


def attend_call(kernel, heads, columns, matmuls, *args):
    rows = args[2].shape[0]
    return pl.pallas_call(
        functools.partial(kernel, heads),
        out_shape=jax.ShapeDtypeStruct((rows, columns), BF),
        compiler_params=pltpu.CompilerParams(vmem_limit_bytes=56 * 1024 * 1024),
        cost_estimate=pl.CostEstimate(
            flops=2 * matmuls * heads * rows * rows * DH, bytes_accessed=8 * rows * columns, transcendentals=heads * rows * rows
        ),
    )(*args)


def finish_kernel(in_ref, q_ref, k_ref, v_ref):
    total = jnp.sum(in_ref[:, 0].astype(F32), axis=0)
    cols = q_ref.shape[1]
    q_ref[...] = total[:, :cols]
    k_ref[...] = total[:, cols : 2 * cols]
    v_ref[...] = total[:, 2 * cols :]


def finish_qkv(v):
    Z, places, R, wide = v.shape
    cols = wide // 3
    out = jax.ShapeDtypeStruct((R, places * cols), F32)
    return pl.pallas_call(
        finish_kernel,
        grid=(places,),
        in_specs=[pl.BlockSpec((Z, 1, R, wide), lambda j: (0, j, 0, 0))],
        out_specs=[pl.BlockSpec((R, cols), lambda j: (0, j))] * 3,
        out_shape=[out] * 3,
    )(v)


def after(values, *others):
    return lax.optimization_barrier((values, others))[0]


def make_body(S, Z):
    every = ("seq", "z", "core")
    join = functools.partial(jnp.concatenate, axis=0)

    def flip(v, axis, size, q):
        return lax.ppermute(v, axis, [(i, i ^ q) for i in range(size)])

    def xor_seq(v, q):
        return flip(v, "seq", S, q)

    def swap_core(v):
        return flip(v, "core", 2, 1)

    def rows(v, block, t):
        return v[block * t : (block + 1) * t]

    def plane_gather(v):
        own = join([v] + [xor_seq(v, q) for q in range(1, S)])
        return own, swap_core(own)

    def plane_scatter(own, other):
        total = own + swap_core(other).astype(F32)
        t = total.shape[0] // S
        got = [xor_seq(rows(total, q, t).astype(BF), q) for q in range(1, S)]
        return rows(total, 0, t), got

    def add_up(mine, got):
        for v in got:
            mine = mine + v.astype(F32)
        return mine

    def exchange(v, axes):
        return lax.all_to_all(v, axes, split_axis=0, concat_axis=0, tiled=True)

    def swap_blocks(v, at, axis, size, me):
        out = v
        for q in range(1, size):
            got = flip(lax.dynamic_index_in_dim(v, me ^ q, at, True), axis, size, q)
            out = lax.dynamic_update_slice_in_dim(out, got, me ^ q, at)
        return out

    def spread_scatter(v, axis, size, me):
        got = [flip(lax.dynamic_index_in_dim(v, me ^ q, 0, False), axis, size, q) for q in range(1, size)]
        return add_up(lax.dynamic_index_in_dim(v, me, 0, False).astype(F32), got)

    def body(
        tokens, segment_ids, pad_mask, cotangent,
        first_gain, first_shift, query_weight, key_weight, value_weight, query_bias, value_bias,
        output_weight, output_bias, second_gain, second_shift, up_weight, up_bias, down_weight, down_bias,
    ):
        s, z, c = (lax.axis_index(a) for a in every)
        n, tp = S * Z * 2, S * 2
        R, D = query_weight.shape
        RF = down_weight.shape[0]
        t = tokens.shape[1]
        L = S * t
        heads_own = H // tp
        cols = D // tp
        half = Z // 2
        both = range(2)

        def lane_blocks(v, order):
            return jnp.concatenate([v[:, i * 2 * R : (i + 1) * 2 * R] for i in order], axis=1)

        natural = [i_s * Z + i_z for i_z in range(Z) for i_s in range(S)]
        back = [natural.index(i) for i in range(S * Z)]

        pieces = [w.reshape(R, tp, cols).transpose(1, 0, 2) for w in (query_weight, key_weight, value_weight)]
        up = up_weight.reshape(R, S, Z, 2, RF).transpose(1, 3, 0, 2, 4).reshape(tp, R, Z * RF)
        mixed = exchange(jnp.concatenate(pieces + [up], axis=2), ("seq", "core")).reshape(tp * R, -1)
        wo = lax.all_gather(output_weight, "z", axis=0)
        wqkv = lax.all_gather(after(mixed[:, : 3 * cols], wo), "z", axis=0, tiled=True)
        wqkv, up = after((wqkv, mixed[:, 3 * cols :]))
        wup = lax.all_gather(up, "z", axis=0, tiled=True)
        wdown = lax.all_gather(after(down_weight, wup), "z", axis=0, tiled=True)
        keep_part = lax.dynamic_slice_in_dim(wo, c * half, half, axis=0)
        got_part = swap_core(lax.dynamic_slice_in_dim(wo, (1 - c) * half, half, axis=0))
        wo = jnp.where(
            c == 0,
            jnp.stack([keep_part, got_part], axis=1),
            jnp.stack([got_part, keep_part], axis=1),
        ).reshape(cols, D)

        small = jnp.concatenate(
            [first_gain, first_shift, query_bias, value_bias, output_bias, second_gain, second_shift, down_bias, up_bias]
        )
        small = exchange(jnp.broadcast_to(after(small, mixed)[None], (n, small.shape[0])), every)
        small = small.astype(F32)
        g1, b1, qb, vb, ob, g2, b2, db = [small[:, i * R : (i + 1) * R].reshape(-1) for i in range(8)]
        ub = small[:, 8 * R :].reshape(S, Z, 2, RF)

        codes = jnp.stack([segment_ids[0], pad_mask[0]])
        codes = jnp.stack([codes] + [xor_seq(codes, q) for q in range(1, S)], axis=1)
        codes = [codes.reshape(2, L), swap_core(codes).reshape(2, L)]
        position = ((s ^ jnp.arange(S, dtype=jnp.int32))[:, None] * t + jnp.arange(t, dtype=jnp.int32)[None]).reshape(L)
        q_info = [jnp.stack([position, code[0]], axis=1) for code in codes]
        k_info = [jnp.stack([position, jnp.where(code[1] == 1, code[0], -1)]) for code in codes]
        keep = pad_mask[0].astype(F32)[:, None]

        xf = tokens[0].astype(F32)
        dy = cotangent[0]
        dyf = dy.astype(F32)
        xhat1, inv1 = normalize(xf)
        normed = plane_gather(lane_blocks((xhat1 * g1 + b1).astype(BF), natural))
        qkv_bias = jnp.stack([qb.reshape(tp, cols), jnp.zeros((tp, cols), F32), vb.reshape(tp, cols)], axis=1)
        qkv_bias = lax.dynamic_index_in_dim(qkv_bias, s * 2 + c, 0, keepdims=False).reshape(3 * cols)
        qkv_out, heads = [None, None], [None, None]
        for e in (1, 0):
            qkv_out[e] = (dot("td,de->te", normed[e], wqkv) + qkv_bias).astype(BF)
            heads[e] = attend_call(attend_kernel, heads_own, cols, 2, q_info[e], k_info[e], qkv_out[e])
        branch = add_up(*plane_scatter(dot("td,de->te", heads[0], wo), dot("td,de->te", heads[1], wo).astype(BF)))
        branch = after(branch, wup)
        middle = xf + (branch + ob) * keep
        xhat2, inv2 = normalize(middle)
        second = plane_gather(lane_blocks((xhat2 * g2 + b2).astype(BF), natural))
        dy_all = plane_gather(after(dy, second[0]))
        up_row = lax.dynamic_index_in_dim(lax.dynamic_index_in_dim(ub, s, 0, False), c, 1, False).reshape(Z * RF)
        active, slope = [None, None], [None, None]
        for e in both:
            hidden = dot("td,df->tf", second[e], wup) + up_row
            phi = 0.5 * (1.0 + lax.erf(hidden * math.sqrt(0.5)))
            slope[e] = phi + hidden * jnp.exp(-0.5 * hidden * hidden) * (1.0 / math.sqrt(2 * math.pi))
            active[e] = (hidden * phi).astype(BF)
        down_grad = dot("tf,td->fd", join(active), join(dy_all)).astype(BF)
        down_grad, wdown = after((down_grad, wdown))
        down_weight_grad = lax.psum_scatter(down_grad, "z", scatter_dimension=0, tiled=True)
        dhidden = [None, None]
        for e in (1, 0):
            dhidden[e] = (dot("td,fd->tf", dy_all[e], wdown) * slope[e]).astype(BF)

        mine, got = plane_scatter(
            dot("tf,df->td", dhidden[0], wup), dot("tf,df->td", dhidden[1], wup).astype(BF)
        )
        fill_dhidden, fill_second = after((dhidden, second), got[0])
        dhidden_join = join(fill_dhidden)
        up_grad = dot("td,tf->df", join(fill_second), dhidden_join).astype(BF)
        mine, got = after((mine, got), up_grad)
        up_grad = lax.psum_scatter(after(up_grad, down_weight_grad), "z", scatter_dimension=0, tiled=True)
        dsecond = lane_blocks(add_up(mine, got), back)
        dmiddle = dyf + norm_back(xhat2, inv2, g2 * dsecond)
        dbranch = (dmiddle * keep).astype(BF)
        dbranch_all = after(plane_gather(dbranch), down_weight_grad)
        dqkv = [None, None]
        for e in both:
            dheads = dot("te,de->td", dbranch_all[e], wo).astype(BF)
            dqkv[e] = attend_call(attend_back_kernel, heads_own, 3 * cols, 5, q_info[e], k_info[e], qkv_out[e], dheads)
        dqkv_join = join(dqkv)
        qkv_grad = dot("td,te->de", join(normed), dqkv_join).astype(BF)
        dqkv, late = after((dqkv, (dbranch_all, heads, active)), qkv_grad)
        qkv_grad = exchange(qkv_grad.reshape(n, R, 3 * cols), ("z", "seq", "core")).reshape(Z, tp, R, 3 * cols)
        mine, got = plane_scatter(dot("te,de->td", dqkv[0], wqkv), dot("te,de->td", dqkv[1], wqkv).astype(BF))
        dbranch_late, heads, active = after(late, got[0])
        wo_grad = dot("td,te->de", join(heads), join(dbranch_late)).astype(BF).reshape(half, 2, R, D)
        keep_part = lax.dynamic_index_in_dim(wo_grad, c, 1, False)
        got_part = swap_core(lax.dynamic_index_in_dim(wo_grad, 1 - c, 1, False))
        wo_grad = jnp.where(c == 0, join([keep_part, got_part]), join([got_part, keep_part]))
        output_weight_grad = spread_scatter(wo_grad, "z", Z, z)
        result = [dot("tf,fd->td", active[0], wdown), dot("tf,fd->td", active[1], wdown).astype(BF)]
        mine, got = after((mine, got), result)
        dnormed = lane_blocks(add_up(mine, got), back)
        input_grad = dmiddle + norm_back(xhat1, inv1, g1 * dnormed)
        block_output = (middle + add_up(*plane_scatter(*result)) + db).astype(BF)
        up_grad = after(up_grad, block_output, output_weight_grad).reshape(S, 2, R, Z * RF)
        up_grad = swap_blocks(swap_blocks(up_grad, 1, "core", 2, c), 0, "seq", S, s)
        up_weight_grad = up_grad.reshape(S, 2, R, Z, RF).transpose(2, 0, 3, 1, 4).reshape(R, -1).astype(F32)
        down_weight_grad = down_weight_grad.astype(F32)
        query_grad, key_grad, value_grad = finish_qkv(qkv_grad)

        bias = jnp.sum(dqkv_join.astype(F32), axis=0).reshape(3, cols)
        spread = jnp.zeros((2, tp, cols), F32)
        spread = lax.dynamic_update_slice(spread, jnp.stack([bias[0], bias[2]])[:, None], (0, s * 2 + c, 0))
        wide = jnp.zeros((S, Z, 2, RF), F32)
        wide = lax.dynamic_update_slice(
            wide, jnp.sum(dhidden_join.astype(F32), axis=0).reshape(1, Z, 1, RF), (s, 0, c, 0)
        )
        vectors = [
            jnp.sum(dbranch.astype(F32), axis=0),
            jnp.sum(dsecond * xhat2, axis=0),
            jnp.sum(dsecond, axis=0),
            jnp.sum(dyf, axis=0),
            wide,
            spread[0],
            spread[1],
            jnp.sum(dnormed * xhat1, axis=0),
            jnp.sum(dnormed, axis=0),
        ]
        packed = jnp.concatenate([v.reshape(S, Z, 2, -1) for v in vectors], axis=3)
        packed = lax.dynamic_index_in_dim(packed, c, 2, False) + swap_core(lax.dynamic_index_in_dim(packed, 1 - c, 2, False))
        packed = spread_scatter(packed, "seq", S, s)
        packed = spread_scatter(packed, "z", Z, z)
        ob_grad, g2_grad, b2_grad, db_grad = [packed[i * R : (i + 1) * R] for i in range(4)]
        ub_grad = packed[4 * R : 4 * R + RF]
        qb_grad, vb_grad, g1_grad, b1_grad = [packed[(4 + i) * R + RF : (5 + i) * R + RF] for i in range(4)]
        return (
            block_output[None], input_grad[None], g1_grad, b1_grad,
            query_grad, key_grad, value_grad, qb_grad, vb_grad,
            output_weight_grad, ob_grad, g2_grad, b2_grad,
            up_weight_grad, ub_grad, down_weight_grad, db_grad,
        )

    return body


def solution(mesh):
    S, DP = mesh.shape["seq"], mesh.shape["dp"]
    Z = DP // 2
    parts = Mesh(mesh.devices.reshape(S, Z, 2), ("seq", "z", "core"))
    every = ("seq", "z", "core")
    token = P(("z", "core"), "seq", None)
    code = P(("z", "core"), "seq")
    vector = P(every)
    matrix = P(every, None)
    return jax.shard_map(
        make_body(S, Z),
        mesh=parts,
        in_specs=(
            token, code, code, token,
            vector, vector, matrix, matrix, matrix, vector, vector,
            matrix, vector, vector, vector, matrix, vector, matrix, vector,
        ),
        out_specs=(
            token, token, vector, vector, matrix, matrix, matrix, vector, vector,
            matrix, vector, vector, vector, matrix, vector, matrix, vector,
        ),
        check_vma=False,
    )
```

```python
import functools
import math

import jax
import jax.numpy as jnp
from jax import lax
from jax.experimental import pallas as pl
from jax.experimental.pallas import tpu as pltpu
from jax.sharding import Mesh
from jax.sharding import PartitionSpec as P

H = 16
DH = 128
EPSILON = 1e-05
NEGATIVE = -1e30
BF = jnp.bfloat16
F32 = jnp.float32
SCALE = 1.0 / math.sqrt(DH)


def dot(form, left, right):
    return jnp.einsum(form, left, right, preferred_element_type=F32)


def normalize(v):
    center = v - jnp.mean(v, axis=-1, keepdims=True)
    inv = lax.rsqrt(jnp.mean(center * center, axis=-1, keepdims=True) + EPSILON)
    return center * inv, inv


def norm_back(xhat, inv, e):
    return (
        e - jnp.mean(e, axis=-1, keepdims=True) - xhat * jnp.mean(e * xhat, axis=-1, keepdims=True)
    ) * inv


def nt(a, b):
    return lax.dot_general(a, b, (((1,), (1,)), ((), ())), preferred_element_type=F32)


def nn(a, b):
    return lax.dot_general(a, b, (((1,), (0,)), ((), ())), preferred_element_type=F32)


def tn(a, b):
    return lax.dot_general(a, b, (((0,), (0,)), ((), ())), preferred_element_type=F32)


def seen(q_ref, k_ref):
    q_pos, q_doc = q_ref[:, 0:1], q_ref[:, 1:2]
    k_pos, k_doc = k_ref[0:1, :], k_ref[1:2, :]
    return ((k_pos <= q_pos) & (k_doc == q_doc)) | (k_pos == q_pos)


def softmax(q, k, visible):
    scores = jnp.where(visible, nt(q, k) * SCALE, NEGATIVE)
    powers = jnp.exp(scores - jnp.max(scores, axis=1, keepdims=True))
    return powers / jnp.sum(powers, axis=1, keepdims=True)


def attend_kernel(heads, q_info, k_info, qkv_ref, out_ref):
    visible = seen(q_info, k_info)
    for h in range(heads):
        q, k, v = (qkv_ref[:, (part * heads + h) * DH : (part * heads + h + 1) * DH] for part in range(3))
        probs = softmax(q, k, visible).astype(BF)
        out_ref[:, h * DH : (h + 1) * DH] = nn(probs, v).astype(BF)


def attend_back_kernel(heads, q_info, k_info, qkv_ref, grad_ref, out_ref):
    visible = seen(q_info, k_info)
    for h in range(heads):
        q, k, v = (qkv_ref[:, (part * heads + h) * DH : (part * heads + h + 1) * DH] for part in range(3))
        grad = grad_ref[:, h * DH : (h + 1) * DH]
        probs = softmax(q, k, visible)
        dp = nt(grad, v)
        delta = jnp.sum(probs * dp, axis=1, keepdims=True)
        dscores = (probs * (dp - delta) * SCALE).astype(BF)
        parts = (nn(dscores, k), tn(dscores, q), tn(probs.astype(BF), grad))
        for part, value in enumerate(parts):
            out_ref[:, (part * heads + h) * DH : (part * heads + h + 1) * DH] = value.astype(BF)


def attend_call(kernel, heads, columns, matmuls, *args):
    rows = args[2].shape[0]
    return pl.pallas_call(
        functools.partial(kernel, heads),
        out_shape=jax.ShapeDtypeStruct((rows, columns), BF),
        compiler_params=pltpu.CompilerParams(vmem_limit_bytes=56 * 1024 * 1024),
        cost_estimate=pl.CostEstimate(
            flops=2 * matmuls * heads * rows * rows * DH, bytes_accessed=8 * rows * columns, transcendentals=heads * rows * rows
        ),
    )(*args)


def finish_kernel(in_ref, q_ref, k_ref, v_ref):
    places, _, wide = in_ref.shape
    cols = wide // 3
    for j in range(places):
        for part, out_ref in enumerate((q_ref, k_ref, v_ref)):
            out_ref[:, j * cols : (j + 1) * cols] = in_ref[j, :, part * cols : (part + 1) * cols].astype(F32)


def finish_qkv(v):
    places, R, wide = v.shape
    out = jax.ShapeDtypeStruct((R, places * wide // 3), F32)
    return pl.pallas_call(finish_kernel, out_shape=[out] * 3)(v)


def spread_kernel(starts, width, in_ref, out_ref):
    for j, row in enumerate(starts):
        for i, to in enumerate(row):
            out_ref[:, to * width : (to + 1) * width] = in_ref[j, :, i * width : (i + 1) * width].astype(F32)


def finish_up(v, S, Z):
    places, R, wide = v.shape
    width = wide // Z
    starts = [[((j // 2) * Z + i) * 2 + j % 2 for i in range(Z)] for j in range(places)]
    if width % 128:
        return v.reshape(S, 2, R, Z, width).transpose(2, 0, 3, 1, 4).reshape(R, -1).astype(F32)
    out = jax.ShapeDtypeStruct((R, places * wide), F32)
    return pl.pallas_call(functools.partial(spread_kernel, starts, width), out_shape=out)(v)


def reorder_kernel(order, in_ref, out_ref):
    width = in_ref.shape[1] // len(order)
    for to, at in enumerate(order):
        out_ref[:, to * width : (to + 1) * width] = in_ref[:, at * width : (at + 1) * width]


def lane_blocks(v, order):
    width = v.shape[1] // len(order)
    if width % 128:
        return jnp.concatenate([v[:, i * width : (i + 1) * width] for i in order], axis=1)
    return pl.pallas_call(
        functools.partial(reorder_kernel, order),
        out_shape=jax.ShapeDtypeStruct(v.shape, v.dtype),
        cost_estimate=pl.CostEstimate(flops=0, bytes_accessed=2 * v.size * v.dtype.itemsize, transcendentals=0),
    )(v)


def after(values, *others):
    return lax.optimization_barrier((values, others))[0]


def make_body(S, Z):
    every = ("seq", "z", "core")
    join = functools.partial(jnp.concatenate, axis=0)

    def flip(v, axis, size, q):
        return lax.ppermute(v, axis, [(i, i ^ q) for i in range(size)])

    def xor_seq(v, q):
        return flip(v, "seq", S, q)

    def swap_core(v):
        return flip(v, "core", 2, 1)

    def rows(v, block, t):
        return v[block * t : (block + 1) * t]

    def plane_gather(v):
        own = join([v] + [xor_seq(v, q) for q in range(1, S)])
        return own, swap_core(own)

    def plane_scatter(own, other):
        total = own + swap_core(other).astype(F32)
        t = total.shape[0] // S
        got = [xor_seq(rows(total, q, t).astype(BF), q) for q in range(1, S)]
        return rows(total, 0, t), got

    def add_up(mine, got):
        for v in got:
            mine = mine + v.astype(F32)
        return mine

    def exchange(v, axes):
        return lax.all_to_all(v, axes, split_axis=0, concat_axis=0, tiled=True)

    def spread_scatter(v, axis, size, me):
        got = [flip(lax.dynamic_index_in_dim(v, me ^ q, 0, False), axis, size, q) for q in range(1, size)]
        return add_up(lax.dynamic_index_in_dim(v, me, 0, False).astype(F32), got)

    def body(
        tokens, segment_ids, pad_mask, cotangent,
        first_gain, first_shift, query_weight, key_weight, value_weight, query_bias, value_bias,
        output_weight, output_bias, second_gain, second_shift, up_weight, up_bias, down_weight, down_bias,
    ):
        s, z, c = (lax.axis_index(a) for a in every)
        n, tp = S * Z * 2, S * 2
        R, D = query_weight.shape
        RF = down_weight.shape[0]
        t = tokens.shape[1]
        L = S * t
        heads_own = H // tp
        cols = D // tp
        half = Z // 2
        both = range(2)

        natural = [i_s * Z + i_z for i_z in range(Z) for i_s in range(S)]
        back = [natural.index(i) for i in range(S * Z)]

        pieces = [w.reshape(R, tp, cols).transpose(1, 0, 2) for w in (query_weight, key_weight, value_weight)]
        up = up_weight.reshape(R, S, Z, 2, RF).transpose(1, 3, 0, 2, 4).reshape(tp, R, Z * RF)
        mixed = exchange(jnp.concatenate(pieces + [up], axis=2), ("seq", "core")).reshape(tp * R, -1)
        wo = lax.all_gather(output_weight, "z", axis=0)
        wqkv = lax.all_gather(after(mixed[:, : 3 * cols], wo), "z", axis=0, tiled=True)
        wqkv, up = after((wqkv, mixed[:, 3 * cols :]))
        wup = lax.all_gather(up, "z", axis=0, tiled=True)
        wdown = lax.all_gather(after(down_weight, wup), "z", axis=0, tiled=True)
        keep_part = lax.dynamic_slice_in_dim(wo, c * half, half, axis=0)
        got_part = swap_core(lax.dynamic_slice_in_dim(wo, (1 - c) * half, half, axis=0))
        wo = jnp.where(
            c == 0,
            jnp.stack([keep_part, got_part], axis=1),
            jnp.stack([got_part, keep_part], axis=1),
        ).reshape(cols, D)

        small = jnp.concatenate(
            [first_gain, first_shift, query_bias, value_bias, output_bias, second_gain, second_shift, down_bias, up_bias]
        )
        small = exchange(jnp.broadcast_to(after(small, mixed)[None], (n, small.shape[0])), every)
        small = small.astype(F32)
        g1, b1, qb, vb, ob, g2, b2, db = [small[:, i * R : (i + 1) * R].reshape(-1) for i in range(8)]
        ub = small[:, 8 * R :].reshape(S, Z, 2, RF)

        codes = jnp.stack([segment_ids[0], pad_mask[0]])
        codes = jnp.stack([codes] + [xor_seq(codes, q) for q in range(1, S)], axis=1)
        codes = [codes.reshape(2, L), swap_core(codes).reshape(2, L)]
        position = ((s ^ jnp.arange(S, dtype=jnp.int32))[:, None] * t + jnp.arange(t, dtype=jnp.int32)[None]).reshape(L)
        q_info = [jnp.stack([position, code[0]], axis=1) for code in codes]
        k_info = [jnp.stack([position, jnp.where(code[1] == 1, code[0], -1)]) for code in codes]
        keep = pad_mask[0].astype(F32)[:, None]

        xf = tokens[0].astype(F32)
        dy = cotangent[0]
        dyf = dy.astype(F32)
        xhat1, inv1 = normalize(xf)
        normed = plane_gather(lane_blocks((xhat1 * g1 + b1).astype(BF), natural))
        qkv_bias = jnp.stack([qb.reshape(tp, cols), jnp.zeros((tp, cols), F32), vb.reshape(tp, cols)], axis=1)
        qkv_bias = lax.dynamic_index_in_dim(qkv_bias, s * 2 + c, 0, keepdims=False).reshape(3 * cols)
        qkv_out, heads = [None, None], [None, None]
        for e in (1, 0):
            qkv_out[e] = (dot("td,de->te", normed[e], wqkv) + qkv_bias).astype(BF)
            heads[e] = attend_call(attend_kernel, heads_own, cols, 2, q_info[e], k_info[e], qkv_out[e])
        branch = add_up(*plane_scatter(dot("td,de->te", heads[0], wo), dot("td,de->te", heads[1], wo).astype(BF)))
        branch = after(branch, wup)
        middle = xf + (branch + ob) * keep
        xhat2, inv2 = normalize(middle)
        second = plane_gather(lane_blocks((xhat2 * g2 + b2).astype(BF), natural))
        dy_all = plane_gather(after(dy, second[0]))
        up_row = lax.dynamic_index_in_dim(lax.dynamic_index_in_dim(ub, s, 0, False), c, 1, False).reshape(Z * RF)
        active, slope = [None, None], [None, None]
        for e in both:
            hidden = dot("td,df->tf", second[e], wup) + up_row
            phi = 0.5 * (1.0 + lax.erf(hidden * math.sqrt(0.5)))
            slope[e] = phi + hidden * jnp.exp(-0.5 * hidden * hidden) * (1.0 / math.sqrt(2 * math.pi))
            active[e] = (hidden * phi).astype(BF)
        down_grad = dot("tf,td->fd", join(active), join(dy_all)).astype(BF)
        down_grad, wdown = after((down_grad, wdown))
        down_weight_grad = lax.psum_scatter(down_grad, "z", scatter_dimension=0, tiled=True)
        dhidden = [None, None]
        for e in (1, 0):
            dhidden[e] = (dot("td,fd->tf", dy_all[e], wdown) * slope[e]).astype(BF)

        mine, got = plane_scatter(
            dot("tf,df->td", dhidden[0], wup), dot("tf,df->td", dhidden[1], wup).astype(BF)
        )
        fill_dhidden, fill_second = after((dhidden, second), got)
        dhidden_join = join(fill_dhidden)
        up_grad = dot("td,tf->df", join(fill_second), dhidden_join).astype(BF)
        up_mm = up_grad
        up_grad = lax.psum_scatter(after(up_grad, down_weight_grad), "z", scatter_dimension=0, tiled=True)
        dsecond = lane_blocks(add_up(mine, got), back)
        active = after(active, up_mm)
        result = dot("tf,fd->td", active[0], wdown) + swap_core(dot("tf,fd->td", active[1], wdown).astype(BF)).astype(F32)
        dsecond = after(dsecond, down_weight_grad, result)
        dmiddle = dyf + norm_back(xhat2, inv2, g2 * dsecond)
        dbranch = (dmiddle * keep).astype(BF)
        dbranch_all = plane_gather(dbranch)
        wo_grad = dot("td,te->de", heads[0], dbranch_all[0]) + dot("td,te->de", heads[1], dbranch_all[1])
        wo_grad = wo_grad.astype(BF).reshape(half, 2, R, D)
        keep_part = lax.dynamic_index_in_dim(wo_grad, c, 1, False)
        got_part = swap_core(lax.dynamic_index_in_dim(wo_grad, 1 - c, 1, False))
        result = after(result, dbranch_all[0])
        result = add_up(rows(result, 0, t), [xor_seq(rows(result, q, t).astype(BF), q) for q in range(1, S)])
        dqkv = [None, None]
        for e in both:
            dheads = dot("te,de->td", dbranch_all[e], wo).astype(BF)
            dqkv[e] = attend_call(attend_back_kernel, heads_own, 3 * cols, 5, q_info[e], k_info[e], qkv_out[e], dheads)
        dqkv_join = after(join(dqkv), result)
        qkv_grad = dot("td,te->de", join(normed), dqkv_join).astype(BF)
        wo_grad = jnp.where(c == 0, join([keep_part, got_part]), join([got_part, keep_part]))
        mixed = jnp.concatenate([after(qkv_grad, up_grad), wo_grad.reshape(D, -1)], axis=1)
        dqkv = after(dqkv, mixed)
        mixed = lax.psum_scatter(after(mixed, up_grad), "z", scatter_dimension=0, tiled=True)
        mixed_sum = mixed
        qkv_grad = exchange(mixed[:, : 3 * cols].reshape(tp, R, 3 * cols), ("seq", "core"))
        output_weight_grad = mixed[:, 3 * cols :].reshape(R, D).astype(F32)
        mine, got = plane_scatter(dot("te,de->td", dqkv[0], wqkv), dot("te,de->td", dqkv[1], wqkv).astype(BF))
        up_grad = exchange(up_grad.reshape(tp, R, Z * RF), ("seq", "core"))
        mine, got = after((mine, got), up_grad)
        dnormed = lane_blocks(add_up(mine, got), back)
        input_grad = dmiddle + norm_back(xhat1, inv1, g1 * dnormed)
        block_output = (middle + result + db).astype(BF)
        up_grad = after(up_grad, mixed_sum)
        up_weight_grad = finish_up(up_grad.reshape(tp, R, Z * RF), S, Z)
        down_weight_grad = down_weight_grad.astype(F32)
        query_grad, key_grad, value_grad = finish_qkv(qkv_grad)

        bias = jnp.sum(dqkv_join.astype(F32), axis=0).reshape(3, cols)
        spread = jnp.zeros((2, tp, cols), F32)
        spread = lax.dynamic_update_slice(spread, jnp.stack([bias[0], bias[2]])[:, None], (0, s * 2 + c, 0))
        wide = jnp.zeros((S, Z, 2, RF), F32)
        wide = lax.dynamic_update_slice(
            wide, jnp.sum(dhidden_join.astype(F32), axis=0).reshape(1, Z, 1, RF), (s, 0, c, 0)
        )
        vectors = [
            jnp.sum(dbranch.astype(F32), axis=0),
            jnp.sum(dsecond * xhat2, axis=0),
            jnp.sum(dsecond, axis=0),
            jnp.sum(dyf, axis=0),
            wide,
            spread[0],
            spread[1],
            jnp.sum(dnormed * xhat1, axis=0),
            jnp.sum(dnormed, axis=0),
        ]
        packed = jnp.concatenate([v.reshape(S, Z, 2, -1) for v in vectors], axis=3)
        packed = lax.dynamic_index_in_dim(packed, c, 2, False) + swap_core(lax.dynamic_index_in_dim(packed, 1 - c, 2, False))
        packed = spread_scatter(packed, "seq", S, s)
        packed = spread_scatter(packed, "z", Z, z)
        ob_grad, g2_grad, b2_grad, db_grad = [packed[i * R : (i + 1) * R] for i in range(4)]
        ub_grad = packed[4 * R : 4 * R + RF]
        qb_grad, vb_grad, g1_grad, b1_grad = [packed[(4 + i) * R + RF : (5 + i) * R + RF] for i in range(4)]
        return (
            block_output[None], input_grad[None], g1_grad, b1_grad,
            query_grad, key_grad, value_grad, qb_grad, vb_grad,
            output_weight_grad, ob_grad, g2_grad, b2_grad,
            up_weight_grad, ub_grad, down_weight_grad, db_grad,
        )

    return body


def solution(mesh):
    S, DP = mesh.shape["seq"], mesh.shape["dp"]
    Z = DP // 2
    parts = Mesh(mesh.devices.reshape(S, Z, 2), ("seq", "z", "core"))
    every = ("seq", "z", "core")
    token = P(("z", "core"), "seq", None)
    code = P(("z", "core"), "seq")
    vector = P(every)
    matrix = P(every, None)
    return jax.shard_map(
        make_body(S, Z),
        mesh=parts,
        in_specs=(
            token, code, code, token,
            vector, vector, matrix, matrix, matrix, vector, vector,
            matrix, vector, vector, vector, matrix, vector, matrix, vector,
        ),
        out_specs=(
            token, token, vector, vector, matrix, matrix, matrix, vector, vector,
            matrix, vector, vector, vector, matrix, vector, matrix, vector,
        ),
        check_vma=False,
    )
```

```python
import functools
import math

import jax
import jax.numpy as jnp
from jax import lax
from jax.experimental import pallas as pl
from jax.experimental.pallas import tpu as pltpu
from jax.sharding import Mesh
from jax.sharding import PartitionSpec as P

H = 16
DH = 128
EPSILON = 1e-05
NEGATIVE = -1e30
BF = jnp.bfloat16
F32 = jnp.float32
SCALE = 1.0 / math.sqrt(DH)


def dot(form, left, right):
    return jnp.einsum(form, left, right, preferred_element_type=F32)


def normalize(v):
    center = v - jnp.mean(v, axis=-1, keepdims=True)
    inv = lax.rsqrt(jnp.mean(center * center, axis=-1, keepdims=True) + EPSILON)
    return center * inv, inv


def norm_back(xhat, inv, e):
    return (
        e - jnp.mean(e, axis=-1, keepdims=True) - xhat * jnp.mean(e * xhat, axis=-1, keepdims=True)
    ) * inv


def nt(a, b):
    return lax.dot_general(a, b, (((1,), (1,)), ((), ())), preferred_element_type=F32)


def nn(a, b):
    return lax.dot_general(a, b, (((1,), (0,)), ((), ())), preferred_element_type=F32)


def tn(a, b):
    return lax.dot_general(a, b, (((0,), (0,)), ((), ())), preferred_element_type=F32)


def seen(q_ref, k_ref):
    q_pos, q_doc = q_ref[:, 0:1], q_ref[:, 1:2]
    k_pos, k_doc = k_ref[0:1, :], k_ref[1:2, :]
    return ((k_pos <= q_pos) & (k_doc == q_doc)) | (k_pos == q_pos)


def softmax(q, k, visible):
    scores = jnp.where(visible, nt(q, k) * SCALE, NEGATIVE)
    powers = jnp.exp(scores - jnp.max(scores, axis=1, keepdims=True))
    return powers / jnp.sum(powers, axis=1, keepdims=True)


def attend_kernel(heads, q_info, k_info, qkv_ref, out_ref):
    visible = seen(q_info, k_info)
    for h in range(heads):
        q, k, v = (qkv_ref[:, (part * heads + h) * DH : (part * heads + h + 1) * DH] for part in range(3))
        probs = softmax(q, k, visible).astype(BF)
        out_ref[:, h * DH : (h + 1) * DH] = nn(probs, v).astype(BF)


def attend_back_kernel(heads, q_info, k_info, qkv_ref, grad_ref, out_ref):
    visible = seen(q_info, k_info)
    for h in range(heads):
        q, k, v = (qkv_ref[:, (part * heads + h) * DH : (part * heads + h + 1) * DH] for part in range(3))
        grad = grad_ref[:, h * DH : (h + 1) * DH]
        probs = softmax(q, k, visible)
        dp = nt(grad, v)
        delta = jnp.sum(probs * dp, axis=1, keepdims=True)
        dscores = (probs * (dp - delta) * SCALE).astype(BF)
        parts = (nn(dscores, k), tn(dscores, q), tn(probs.astype(BF), grad))
        for part, value in enumerate(parts):
            out_ref[:, (part * heads + h) * DH : (part * heads + h + 1) * DH] = value.astype(BF)


def attend_call(kernel, heads, columns, matmuls, *args):
    rows = args[2].shape[0]
    return pl.pallas_call(
        functools.partial(kernel, heads),
        out_shape=jax.ShapeDtypeStruct((rows, columns), BF),
        compiler_params=pltpu.CompilerParams(vmem_limit_bytes=56 * 1024 * 1024),
        cost_estimate=pl.CostEstimate(
            flops=2 * matmuls * heads * rows * rows * DH, bytes_accessed=8 * rows * columns, transcendentals=heads * rows * rows
        ),
    )(*args)


def finish_kernel(in_ref, q_ref, k_ref, v_ref):
    places, _, wide = in_ref.shape
    cols = wide // 3
    for j in range(places):
        for part, out_ref in enumerate((q_ref, k_ref, v_ref)):
            out_ref[:, j * cols : (j + 1) * cols] = in_ref[j, :, part * cols : (part + 1) * cols].astype(F32)


def finish_qkv(v):
    places, R, wide = v.shape
    out = jax.ShapeDtypeStruct((R, places * wide // 3), F32)
    return pl.pallas_call(finish_kernel, out_shape=[out] * 3)(v)


def spread_kernel(starts, width, in_ref, out_ref):
    for j, row in enumerate(starts):
        for i, to in enumerate(row):
            out_ref[:, to * width : (to + 1) * width] = in_ref[j, :, i * width : (i + 1) * width].astype(F32)


def finish_up(v, S, Z):
    places, R, wide = v.shape
    width = wide // Z
    starts = [[((j // 2) * Z + i) * 2 + j % 2 for i in range(Z)] for j in range(places)]
    if width % 128:
        return v.reshape(S, 2, R, Z, width).transpose(2, 0, 3, 1, 4).reshape(R, -1).astype(F32)
    out = jax.ShapeDtypeStruct((R, places * wide), F32)
    return pl.pallas_call(functools.partial(spread_kernel, starts, width), out_shape=out)(v)


def reorder_kernel(order, in_ref, out_ref):
    width = in_ref.shape[1] // len(order)
    for to, at in enumerate(order):
        out_ref[:, to * width : (to + 1) * width] = in_ref[:, at * width : (at + 1) * width]


def lane_blocks(v, order):
    width = v.shape[1] // len(order)
    if width % 128:
        return jnp.concatenate([v[:, i * width : (i + 1) * width] for i in order], axis=1)
    return pl.pallas_call(
        functools.partial(reorder_kernel, order),
        out_shape=jax.ShapeDtypeStruct(v.shape, v.dtype),
        cost_estimate=pl.CostEstimate(flops=0, bytes_accessed=2 * v.size * v.dtype.itemsize, transcendentals=0),
    )(v)


def after(values, *others):
    return lax.optimization_barrier((values, others))[0]


def make_body(S, Z):
    every = ("seq", "z", "core")
    join = functools.partial(jnp.concatenate, axis=0)

    def flip(v, axis, size, q):
        return lax.ppermute(v, axis, [(i, i ^ q) for i in range(size)])

    def xor_seq(v, q):
        return flip(v, "seq", S, q)

    def swap_core(v):
        return flip(v, "core", 2, 1)

    def rows(v, block, t):
        return v[block * t : (block + 1) * t]

    def plane_gather(v):
        own = join([v] + [xor_seq(v, q) for q in range(1, S)])
        return own, swap_core(own)

    def plane_scatter(own, other):
        total = own + swap_core(other).astype(F32)
        t = total.shape[0] // S
        got = [xor_seq(rows(total, q, t).astype(BF), q) for q in range(1, S)]
        return rows(total, 0, t), got

    def add_up(mine, got):
        for v in got:
            mine = mine + v.astype(F32)
        return mine

    def exchange(v, axes):
        return lax.all_to_all(v, axes, split_axis=0, concat_axis=0, tiled=True)

    def spread_scatter(v, axis, size, me):
        got = [flip(lax.dynamic_index_in_dim(v, me ^ q, 0, False), axis, size, q) for q in range(1, size)]
        return add_up(lax.dynamic_index_in_dim(v, me, 0, False).astype(F32), got)

    def body(
        tokens, segment_ids, pad_mask, cotangent,
        first_gain, first_shift, query_weight, key_weight, value_weight, query_bias, value_bias,
        output_weight, output_bias, second_gain, second_shift, up_weight, up_bias, down_weight, down_bias,
    ):
        s, z, c = (lax.axis_index(a) for a in every)
        n, tp = S * Z * 2, S * 2
        R, D = query_weight.shape
        RF = down_weight.shape[0]
        t = tokens.shape[1]
        L = S * t
        heads_own = H // tp
        cols = D // tp
        half = Z // 2
        both = range(2)

        natural = [i_s * Z + i_z for i_z in range(Z) for i_s in range(S)]
        back = [natural.index(i) for i in range(S * Z)]

        pieces = [w.reshape(R, tp, cols).transpose(1, 0, 2) for w in (query_weight, key_weight, value_weight)]
        up = up_weight.reshape(R, S, Z, 2, RF).transpose(1, 3, 0, 2, 4).reshape(tp, R, Z * RF)
        qkv = exchange(jnp.concatenate(pieces, axis=2), ("seq", "core")).reshape(tp * R, 3 * cols)
        small = jnp.concatenate(
            [first_gain, first_shift, query_bias, value_bias, output_bias, second_gain, second_shift, down_bias, up_bias]
        )
        small = exchange(jnp.broadcast_to(after(small, qkv)[None], (n, small.shape[0])), every)
        small_there = small
        small = small.astype(F32)
        g1, b1, qb, vb, ob, g2, b2, db = [small[:, i * R : (i + 1) * R].reshape(-1) for i in range(8)]
        ub = small[:, 8 * R :].reshape(S, Z, 2, RF)

        wo = lax.all_gather(output_weight, "z", axis=0)
        wqkv = lax.all_gather(after(qkv, wo), "z", axis=0, tiled=True)
        up = exchange(after(up, small_there), ("seq", "core")).reshape(tp * R, Z * RF)
        wqkv, up = after((wqkv, up))
        wup = lax.all_gather(up, "z", axis=0, tiled=True)
        wdown = lax.all_gather(after(down_weight, wup), "z", axis=0, tiled=True)
        keep_part = lax.dynamic_slice_in_dim(wo, c * half, half, axis=0)
        got_part = swap_core(lax.dynamic_slice_in_dim(wo, (1 - c) * half, half, axis=0))
        wo = jnp.where(
            c == 0,
            jnp.stack([keep_part, got_part], axis=1),
            jnp.stack([got_part, keep_part], axis=1),
        ).reshape(cols, D)

        codes = jnp.stack([segment_ids[0], pad_mask[0]])
        codes = jnp.stack([codes] + [xor_seq(codes, q) for q in range(1, S)], axis=1)
        codes = [codes.reshape(2, L), swap_core(codes).reshape(2, L)]
        position = ((s ^ jnp.arange(S, dtype=jnp.int32))[:, None] * t + jnp.arange(t, dtype=jnp.int32)[None]).reshape(L)
        q_info = [jnp.stack([position, code[0]], axis=1) for code in codes]
        k_info = [jnp.stack([position, jnp.where(code[1] == 1, code[0], -1)]) for code in codes]
        keep = pad_mask[0].astype(F32)[:, None]

        xf = tokens[0].astype(F32)
        dy = cotangent[0]
        dyf = dy.astype(F32)
        xhat1, inv1 = normalize(xf)
        normed = plane_gather(lane_blocks((xhat1 * g1 + b1).astype(BF), natural))
        qkv_bias = jnp.stack([qb.reshape(tp, cols), jnp.zeros((tp, cols), F32), vb.reshape(tp, cols)], axis=1)
        qkv_bias = lax.dynamic_index_in_dim(qkv_bias, s * 2 + c, 0, keepdims=False).reshape(3 * cols)
        qkv_out, heads = [None, None], [None, None]
        for e in (1, 0):
            qkv_out[e] = (dot("td,de->te", normed[e], wqkv) + qkv_bias).astype(BF)
            heads[e] = attend_call(attend_kernel, heads_own, cols, 2, q_info[e], k_info[e], qkv_out[e])
        branch = add_up(*plane_scatter(dot("td,de->te", heads[0], wo), dot("td,de->te", heads[1], wo).astype(BF)))
        branch = after(branch, wup)
        middle = xf + (branch + ob) * keep
        xhat2, inv2 = normalize(middle)
        second = plane_gather(lane_blocks((xhat2 * g2 + b2).astype(BF), natural))
        dy_all = plane_gather(after(dy, second[0]))
        up_row = lax.dynamic_index_in_dim(lax.dynamic_index_in_dim(ub, s, 0, False), c, 1, False).reshape(Z * RF)
        active, slope = [None, None], [None, None]
        for e in both:
            hidden = dot("td,df->tf", second[e], wup) + up_row
            phi = 0.5 * (1.0 + lax.erf(hidden * math.sqrt(0.5)))
            slope[e] = phi + hidden * jnp.exp(-0.5 * hidden * hidden) * (1.0 / math.sqrt(2 * math.pi))
            active[e] = (hidden * phi).astype(BF)
        down_grad = dot("tf,td->fd", join(active), join(dy_all)).astype(BF)
        down_grad, wdown = after((down_grad, wdown))
        down_weight_grad = lax.psum_scatter(down_grad, "z", scatter_dimension=0, tiled=True)
        dhidden = [None, None]
        for e in (1, 0):
            dhidden[e] = (dot("td,fd->tf", dy_all[e], wdown) * slope[e]).astype(BF)

        mine, got = plane_scatter(
            dot("tf,df->td", dhidden[0], wup), dot("tf,df->td", dhidden[1], wup).astype(BF)
        )
        fill_dhidden, fill_second = after((dhidden, second), got)
        dhidden_join = join(fill_dhidden)
        up_grad = dot("td,tf->df", join(fill_second), dhidden_join).astype(BF)
        up_mm = up_grad
        up_grad = lax.psum_scatter(after(up_grad, down_weight_grad), "z", scatter_dimension=0, tiled=True)
        dsecond = lane_blocks(add_up(mine, got), back)
        dsecond = after(dsecond, down_weight_grad, up_mm)
        dmiddle = dyf + norm_back(xhat2, inv2, g2 * dsecond)
        dbranch = (dmiddle * keep).astype(BF)
        dbranch_all = plane_gather(dbranch)
        active = after(active, dbranch)
        result = dot("tf,fd->td", active[0], wdown) + swap_core(dot("tf,fd->td", active[1], wdown).astype(BF)).astype(F32)
        wo_grad = dot("td,te->de", heads[0], dbranch_all[0]) + dot("td,te->de", heads[1], dbranch_all[1])
        wo_grad = wo_grad.astype(BF).reshape(half, 2, R, D)
        keep_part = lax.dynamic_index_in_dim(wo_grad, c, 1, False)
        got_part = swap_core(lax.dynamic_index_in_dim(wo_grad, 1 - c, 1, False))
        result, dbranch_all = after((result, dbranch_all))
        result_got = [xor_seq(rows(result, q, t).astype(BF), q) for q in range(1, S)]
        dqkv = [None, None]
        for e in both:
            dheads = dot("te,de->td", dbranch_all[e], wo).astype(BF)
            dqkv[e] = attend_call(attend_back_kernel, heads_own, 3 * cols, 5, q_info[e], k_info[e], qkv_out[e], dheads)
        qkv_grad = (dot("td,te->de", normed[0], dqkv[0]) + dot("td,te->de", normed[1], dqkv[1])).astype(BF)
        wo_grad = jnp.where(c == 0, join([keep_part, got_part]), join([got_part, keep_part]))
        result = add_up(rows(result, 0, t), after(result_got, qkv_grad))
        mixed = jnp.concatenate([qkv_grad, wo_grad.reshape(D, -1)], axis=1)
        dqkv = after(dqkv, mixed)
        mixed = lax.psum_scatter(after(mixed, up_grad, result_got), "z", scatter_dimension=0, tiled=True)
        mixed_sum = mixed
        qkv_grad = exchange(mixed[:, : 3 * cols].reshape(tp, R, 3 * cols), ("seq", "core"))
        output_weight_grad = mixed[:, 3 * cols :].reshape(R, D).astype(F32)
        mine, got = plane_scatter(dot("te,de->td", dqkv[0], wqkv), dot("te,de->td", dqkv[1], wqkv).astype(BF))
        up_grad = exchange(up_grad.reshape(tp, R, Z * RF), ("seq", "core"))
        mine, got = after((mine, got), up_grad)
        dnormed = lane_blocks(add_up(mine, got), back)
        input_grad = dmiddle + norm_back(xhat1, inv1, g1 * dnormed)
        block_output = (middle + result + db).astype(BF)
        up_grad = after(up_grad, mixed_sum)
        up_weight_grad = finish_up(up_grad.reshape(tp, R, Z * RF), S, Z)
        down_weight_grad = down_weight_grad.astype(F32)
        query_grad, key_grad, value_grad = finish_qkv(qkv_grad)

        bias = sum(jnp.sum(v.astype(F32), axis=0) for v in dqkv).reshape(3, cols)
        spread = jnp.zeros((2, tp, cols), F32)
        spread = lax.dynamic_update_slice(spread, jnp.stack([bias[0], bias[2]])[:, None], (0, s * 2 + c, 0))
        wide = jnp.zeros((S, Z, 2, RF), F32)
        wide = lax.dynamic_update_slice(
            wide, jnp.sum(dhidden_join.astype(F32), axis=0).reshape(1, Z, 1, RF), (s, 0, c, 0)
        )
        vectors = [
            jnp.sum(dbranch.astype(F32), axis=0),
            jnp.sum(dsecond * xhat2, axis=0),
            jnp.sum(dsecond, axis=0),
            jnp.sum(dyf, axis=0),
            wide,
            spread[0],
            spread[1],
            jnp.sum(dnormed * xhat1, axis=0),
            jnp.sum(dnormed, axis=0),
        ]
        packed = jnp.concatenate([v.reshape(S, Z, 2, -1) for v in vectors], axis=3)
        packed = lax.dynamic_index_in_dim(packed, c, 2, False) + swap_core(lax.dynamic_index_in_dim(packed, 1 - c, 2, False))
        packed = spread_scatter(packed, "seq", S, s)
        packed = spread_scatter(packed, "z", Z, z)
        ob_grad, g2_grad, b2_grad, db_grad = [packed[i * R : (i + 1) * R] for i in range(4)]
        ub_grad = packed[4 * R : 4 * R + RF]
        qb_grad, vb_grad, g1_grad, b1_grad = [packed[(4 + i) * R + RF : (5 + i) * R + RF] for i in range(4)]
        return (
            block_output[None], input_grad[None], g1_grad, b1_grad,
            query_grad, key_grad, value_grad, qb_grad, vb_grad,
            output_weight_grad, ob_grad, g2_grad, b2_grad,
            up_weight_grad, ub_grad, down_weight_grad, db_grad,
        )

    return body


def solution(mesh):
    S, DP = mesh.shape["seq"], mesh.shape["dp"]
    Z = DP // 2
    parts = Mesh(mesh.devices.reshape(S, Z, 2), ("seq", "z", "core"))
    every = ("seq", "z", "core")
    token = P(("z", "core"), "seq", None)
    code = P(("z", "core"), "seq")
    vector = P(every)
    matrix = P(every, None)
    return jax.shard_map(
        make_body(S, Z),
        mesh=parts,
        in_specs=(
            token, code, code, token,
            vector, vector, matrix, matrix, matrix, vector, vector,
            matrix, vector, vector, vector, matrix, vector, matrix, vector,
        ),
        out_specs=(
            token, token, vector, vector, matrix, matrix, matrix, vector, vector,
            matrix, vector, vector, vector, matrix, vector, matrix, vector,
        ),
        check_vma=False,
    )
```

```python
import functools
import math

import jax
import jax.numpy as jnp
from jax import lax
from jax.experimental import pallas as pl
from jax.experimental.pallas import tpu as pltpu
from jax.sharding import Mesh
from jax.sharding import PartitionSpec as P

H = 16
DH = 128
EPSILON = 1e-05
NEGATIVE = -1e30
BF = jnp.bfloat16
F32 = jnp.float32
SCALE = 1.0 / math.sqrt(DH)


def dot(form, left, right):
    return jnp.einsum(form, left, right, preferred_element_type=F32)


def normalize(v):
    center = v - jnp.mean(v, axis=-1, keepdims=True)
    inv = lax.rsqrt(jnp.mean(center * center, axis=-1, keepdims=True) + EPSILON)
    return center * inv, inv


def norm_back(xhat, inv, e):
    return (
        e - jnp.mean(e, axis=-1, keepdims=True) - xhat * jnp.mean(e * xhat, axis=-1, keepdims=True)
    ) * inv


def nt(a, b):
    return lax.dot_general(a, b, (((1,), (1,)), ((), ())), preferred_element_type=F32)


def nn(a, b):
    return lax.dot_general(a, b, (((1,), (0,)), ((), ())), preferred_element_type=F32)


def tn(a, b):
    return lax.dot_general(a, b, (((0,), (0,)), ((), ())), preferred_element_type=F32)


def seen(q_ref, k_ref):
    q_pos, q_doc = q_ref[:, 0:1], q_ref[:, 1:2]
    k_pos, k_doc = k_ref[0:1, :], k_ref[1:2, :]
    return ((k_pos <= q_pos) & (k_doc == q_doc)) | (k_pos == q_pos)


def softmax(q, k, visible):
    scores = jnp.where(visible, nt(q, k) * SCALE, NEGATIVE)
    powers = jnp.exp(scores - jnp.max(scores, axis=1, keepdims=True))
    return powers / jnp.sum(powers, axis=1, keepdims=True)


def attend_kernel(heads, q_info, k_info, qkv_ref, out_ref):
    visible = seen(q_info, k_info)
    for h in range(heads):
        q, k, v = (qkv_ref[:, (part * heads + h) * DH : (part * heads + h + 1) * DH] for part in range(3))
        probs = softmax(q, k, visible).astype(BF)
        out_ref[:, h * DH : (h + 1) * DH] = nn(probs, v).astype(BF)


def attend_back_kernel(heads, q_info, k_info, qkv_ref, grad_ref, out_ref):
    visible = seen(q_info, k_info)
    for h in range(heads):
        q, k, v = (qkv_ref[:, (part * heads + h) * DH : (part * heads + h + 1) * DH] for part in range(3))
        grad = grad_ref[:, h * DH : (h + 1) * DH]
        probs = softmax(q, k, visible)
        dp = nt(grad, v)
        delta = jnp.sum(probs * dp, axis=1, keepdims=True)
        dscores = (probs * (dp - delta) * SCALE).astype(BF)
        parts = (nn(dscores, k), tn(dscores, q), tn(probs.astype(BF), grad))
        for part, value in enumerate(parts):
            out_ref[:, (part * heads + h) * DH : (part * heads + h + 1) * DH] = value.astype(BF)


def attend_call(kernel, heads, columns, matmuls, *args):
    rows = args[2].shape[0]
    return pl.pallas_call(
        functools.partial(kernel, heads),
        out_shape=jax.ShapeDtypeStruct((rows, columns), BF),
        compiler_params=pltpu.CompilerParams(vmem_limit_bytes=56 * 1024 * 1024),
        cost_estimate=pl.CostEstimate(
            flops=2 * matmuls * heads * rows * rows * DH, bytes_accessed=8 * rows * columns, transcendentals=heads * rows * rows
        ),
    )(*args)


def finish_kernel(in_ref, q_ref, k_ref, v_ref):
    places, _, wide = in_ref.shape
    cols = wide // 3
    for j in range(places):
        for part, out_ref in enumerate((q_ref, k_ref, v_ref)):
            out_ref[:, j * cols : (j + 1) * cols] = in_ref[j, :, part * cols : (part + 1) * cols].astype(F32)


def finish_qkv(v):
    places, R, wide = v.shape
    out = jax.ShapeDtypeStruct((R, places * wide // 3), F32)
    return pl.pallas_call(finish_kernel, out_shape=[out] * 3)(v)


def spread_kernel(starts, width, in_ref, out_ref):
    for j, row in enumerate(starts):
        for i, to in enumerate(row):
            out_ref[:, to * width : (to + 1) * width] = in_ref[j, :, i * width : (i + 1) * width].astype(F32)


def finish_up(v, S, Z):
    places, R, wide = v.shape
    width = wide // Z
    starts = [[((j // 2) * Z + i) * 2 + j % 2 for i in range(Z)] for j in range(places)]
    if width % 128:
        return v.reshape(S, 2, R, Z, width).transpose(2, 0, 3, 1, 4).reshape(R, -1).astype(F32)
    out = jax.ShapeDtypeStruct((R, places * wide), F32)
    return pl.pallas_call(functools.partial(spread_kernel, starts, width), out_shape=out)(v)


def reorder_kernel(order, in_ref, out_ref):
    width = in_ref.shape[1] // len(order)
    for to, at in enumerate(order):
        out_ref[:, to * width : (to + 1) * width] = in_ref[:, at * width : (at + 1) * width]


def lane_blocks(v, order):
    width = v.shape[1] // len(order)
    if width % 128:
        return jnp.concatenate([v[:, i * width : (i + 1) * width] for i in order], axis=1)
    return pl.pallas_call(
        functools.partial(reorder_kernel, order),
        out_shape=jax.ShapeDtypeStruct(v.shape, v.dtype),
        cost_estimate=pl.CostEstimate(flops=0, bytes_accessed=2 * v.size * v.dtype.itemsize, transcendentals=0),
    )(v)


def after(values, *others):
    return lax.optimization_barrier((values, others))[0]


def make_body(S, Z):
    every = ("seq", "z", "core")
    join = functools.partial(jnp.concatenate, axis=0)

    def flip(v, axis, size, q):
        return lax.ppermute(v, axis, [(i, i ^ q) for i in range(size)])

    def xor_seq(v, q):
        return flip(v, "seq", S, q)

    def swap_core(v):
        return flip(v, "core", 2, 1)

    def rows(v, block, t):
        return v[block * t : (block + 1) * t]

    def plane_gather(v):
        own = join([v] + [xor_seq(v, q) for q in range(1, S)])
        return own, swap_core(own)

    def plane_scatter(own, other):
        total = own + swap_core(other).astype(F32)
        t = total.shape[0] // S
        got = [xor_seq(rows(total, q, t).astype(BF), q) for q in range(1, S)]
        return rows(total, 0, t), got

    def add_up(mine, got):
        for v in got:
            mine = mine + v.astype(F32)
        return mine

    def exchange(v, axes):
        return lax.all_to_all(v, axes, split_axis=0, concat_axis=0, tiled=True)

    def spread_scatter(v, axis, size, me):
        got = [flip(lax.dynamic_index_in_dim(v, me ^ q, 0, False), axis, size, q) for q in range(1, size)]
        return add_up(lax.dynamic_index_in_dim(v, me, 0, False).astype(F32), got)

    def body(
        tokens, segment_ids, pad_mask, cotangent,
        first_gain, first_shift, query_weight, key_weight, value_weight, query_bias, value_bias,
        output_weight, output_bias, second_gain, second_shift, up_weight, up_bias, down_weight, down_bias,
    ):
        s, z, c = (lax.axis_index(a) for a in every)
        n, tp = S * Z * 2, S * 2
        R, D = query_weight.shape
        RF = down_weight.shape[0]
        t = tokens.shape[1]
        L = S * t
        heads_own = H // tp
        cols = D // tp
        half = Z // 2
        both = range(2)

        natural = [i_s * Z + i_z for i_z in range(Z) for i_s in range(S)]
        back = [natural.index(i) for i in range(S * Z)]

        pieces = [w.reshape(R, tp, cols).transpose(1, 0, 2) for w in (query_weight, key_weight, value_weight)]
        up = up_weight.reshape(R, S, Z, 2, RF).transpose(1, 3, 0, 2, 4).reshape(tp, R, Z * RF)
        qkv = exchange(jnp.concatenate(pieces, axis=2), ("seq", "core")).reshape(tp * R, 3 * cols)
        small = jnp.concatenate(
            [first_gain, first_shift, query_bias, value_bias, output_bias, second_gain, second_shift, down_bias, up_bias]
        )
        small = exchange(jnp.broadcast_to(after(small, qkv)[None], (n, small.shape[0])), every)
        small_there = small
        small = small.astype(F32)
        g1, b1, qb, vb, ob, g2, b2, db = [small[:, i * R : (i + 1) * R].reshape(-1) for i in range(8)]
        ub = small[:, 8 * R :].reshape(S, Z, 2, RF)

        wo = lax.all_gather(output_weight, "z", axis=0)
        wqkv = lax.all_gather(after(qkv, wo), "z", axis=0, tiled=True)
        up = exchange(after(up, small_there), ("seq", "core")).reshape(tp * R, Z * RF)
        wqkv, up = after((wqkv, up))
        wup = lax.all_gather(up, "z", axis=0, tiled=True)
        wdown = lax.all_gather(after(down_weight, wup), "z", axis=0, tiled=True)
        keep_part = lax.dynamic_slice_in_dim(wo, c * half, half, axis=0)
        got_part = swap_core(lax.dynamic_slice_in_dim(wo, (1 - c) * half, half, axis=0))
        wo = jnp.where(
            c == 0,
            jnp.stack([keep_part, got_part], axis=1),
            jnp.stack([got_part, keep_part], axis=1),
        ).reshape(cols, D)

        codes = jnp.stack([segment_ids[0], pad_mask[0]])
        codes = jnp.stack([codes] + [xor_seq(codes, q) for q in range(1, S)], axis=1)
        codes = [codes.reshape(2, L), swap_core(codes).reshape(2, L)]
        position = ((s ^ jnp.arange(S, dtype=jnp.int32))[:, None] * t + jnp.arange(t, dtype=jnp.int32)[None]).reshape(L)
        q_info = [jnp.stack([position, code[0]], axis=1) for code in codes]
        k_info = [jnp.stack([position, jnp.where(code[1] == 1, code[0], -1)]) for code in codes]
        keep = pad_mask[0].astype(F32)[:, None]

        xf = tokens[0].astype(F32)
        dy = cotangent[0]
        dyf = dy.astype(F32)
        xhat1, inv1 = normalize(xf)
        normed = plane_gather(lane_blocks((xhat1 * g1 + b1).astype(BF), natural))
        qkv_bias = jnp.stack([qb.reshape(tp, cols), jnp.zeros((tp, cols), F32), vb.reshape(tp, cols)], axis=1)
        qkv_bias = lax.dynamic_index_in_dim(qkv_bias, s * 2 + c, 0, keepdims=False).reshape(3 * cols)
        qkv_out, heads = [None, None], [None, None]
        for e in (1, 0):
            qkv_out[e] = (dot("td,de->te", normed[e], wqkv) + qkv_bias).astype(BF)
            heads[e] = attend_call(attend_kernel, heads_own, cols, 2, q_info[e], k_info[e], qkv_out[e])
        branch = add_up(*plane_scatter(dot("td,de->te", heads[0], wo), dot("td,de->te", heads[1], wo).astype(BF)))
        branch = after(branch, wup)
        middle = xf + (branch + ob) * keep
        xhat2, inv2 = normalize(middle)
        second = plane_gather(lane_blocks((xhat2 * g2 + b2).astype(BF), natural))
        dy_all = plane_gather(after(dy, second[0]))
        up_row = lax.dynamic_index_in_dim(lax.dynamic_index_in_dim(ub, s, 0, False), c, 1, False).reshape(Z * RF)
        active, slope = [None, None], [None, None]
        for e in both:
            hidden = dot("td,df->tf", second[e], wup) + up_row
            phi = 0.5 * (1.0 + lax.erf(hidden * math.sqrt(0.5)))
            slope[e] = phi + hidden * jnp.exp(-0.5 * hidden * hidden) * (1.0 / math.sqrt(2 * math.pi))
            active[e] = (hidden * phi).astype(BF)
        early = D - D // 4
        active_join, dy_join = join(active), join(dy_all)
        down_grad = dot("tf,td->fd", active_join, dy_join[:, :early]).astype(BF)
        down_grad, wdown = after((down_grad, wdown))
        down_early = lax.psum_scatter(down_grad, "z", scatter_dimension=0, tiled=True)
        dhidden = [None, None]
        for e in (1, 0):
            dhidden[e] = (dot("td,fd->tf", dy_all[e], wdown) * slope[e]).astype(BF)

        mine, got = plane_scatter(
            dot("tf,df->td", dhidden[0], wup), dot("tf,df->td", dhidden[1], wup).astype(BF)
        )
        fill_dhidden, fill_second = after((dhidden, second), got)
        dhidden_join = join(fill_dhidden)
        up_grad = dot("td,tf->df", join(fill_second), dhidden_join).astype(BF)
        up_mm = up_grad
        active_join, dy_join = after((active_join, dy_join), up_mm)
        down_rest = dot("tf,td->fd", active_join, dy_join[:, early:]).astype(BF)
        up_grad = lax.psum_scatter(after(up_grad, down_early), "z", scatter_dimension=0, tiled=True)
        dsecond = lane_blocks(add_up(mine, got), back)
        dsecond = after(dsecond, down_early, up_mm, down_rest)
        dmiddle = dyf + norm_back(xhat2, inv2, g2 * dsecond)
        dbranch = (dmiddle * keep).astype(BF)
        dbranch_all = plane_gather(dbranch)
        active = after(active, dbranch)
        result = dot("tf,fd->td", active[0], wdown) + swap_core(dot("tf,fd->td", active[1], wdown).astype(BF)).astype(F32)
        wo_grad = dot("td,te->de", heads[0], dbranch_all[0]) + dot("td,te->de", heads[1], dbranch_all[1])
        wo_grad = wo_grad.astype(BF).reshape(half, 2, R, D)
        keep_part = lax.dynamic_index_in_dim(wo_grad, c, 1, False)
        got_part = swap_core(lax.dynamic_index_in_dim(wo_grad, 1 - c, 1, False))
        result, dbranch_all = after((result, dbranch_all))
        result_got = [xor_seq(rows(result, q, t).astype(BF), q) for q in range(1, S)]
        dqkv = [None, None]
        for e in both:
            dheads = dot("te,de->td", dbranch_all[e], wo).astype(BF)
            dqkv[e] = attend_call(attend_back_kernel, heads_own, 3 * cols, 5, q_info[e], k_info[e], qkv_out[e], dheads)
        qkv_grad = (dot("td,te->de", normed[0], dqkv[0]) + dot("td,te->de", normed[1], dqkv[1])).astype(BF)
        wo_grad = jnp.where(c == 0, join([keep_part, got_part]), join([got_part, keep_part]))
        result = add_up(rows(result, 0, t), after(result_got, qkv_grad))
        mixed = jnp.concatenate([qkv_grad, wo_grad.reshape(D, -1)], axis=1)
        dqkv = after(dqkv, mixed)
        mixed = lax.psum_scatter(after(mixed, up_grad, result_got), "z", scatter_dimension=0, tiled=True)
        mixed_sum = mixed
        qkv_grad = exchange(mixed[:, : 3 * cols].reshape(tp, R, 3 * cols), ("seq", "core"))
        output_weight_grad = mixed[:, 3 * cols :].reshape(R, D).astype(F32)
        mine, got = plane_scatter(dot("te,de->td", dqkv[0], wqkv), dot("te,de->td", dqkv[1], wqkv).astype(BF))
        up_grad = exchange(up_grad.reshape(tp, R, Z * RF), ("seq", "core"))
        mine, got = after((mine, got), up_grad)
        dnormed = lane_blocks(add_up(mine, got), back)
        input_grad = dmiddle + norm_back(xhat1, inv1, g1 * dnormed)
        block_output = (middle + result + db).astype(BF)
        up_grad = after(up_grad, mixed_sum)
        up_weight_grad = finish_up(up_grad.reshape(tp, R, Z * RF), S, Z)
        down_rest = lax.psum_scatter(after(down_rest, mixed_sum), "z", scatter_dimension=0, tiled=True)
        down_weight_grad = jnp.concatenate([down_early, down_rest], axis=1).astype(F32)
        query_grad, key_grad, value_grad = finish_qkv(qkv_grad)

        bias = sum(jnp.sum(v.astype(F32), axis=0) for v in dqkv).reshape(3, cols)
        spread = jnp.zeros((2, tp, cols), F32)
        spread = lax.dynamic_update_slice(spread, jnp.stack([bias[0], bias[2]])[:, None], (0, s * 2 + c, 0))
        wide = jnp.zeros((S, Z, 2, RF), F32)
        wide = lax.dynamic_update_slice(
            wide, jnp.sum(dhidden_join.astype(F32), axis=0).reshape(1, Z, 1, RF), (s, 0, c, 0)
        )
        vectors = [
            jnp.sum(dbranch.astype(F32), axis=0),
            jnp.sum(dsecond * xhat2, axis=0),
            jnp.sum(dsecond, axis=0),
            jnp.sum(dyf, axis=0),
            wide,
            spread[0],
            spread[1],
            jnp.sum(dnormed * xhat1, axis=0),
            jnp.sum(dnormed, axis=0),
        ]
        packed = jnp.concatenate([v.reshape(S, Z, 2, -1) for v in vectors], axis=3)
        packed = lax.dynamic_index_in_dim(packed, c, 2, False) + swap_core(lax.dynamic_index_in_dim(packed, 1 - c, 2, False))
        packed = spread_scatter(packed, "seq", S, s)
        packed = spread_scatter(packed, "z", Z, z)
        ob_grad, g2_grad, b2_grad, db_grad = [packed[i * R : (i + 1) * R] for i in range(4)]
        ub_grad = packed[4 * R : 4 * R + RF]
        qb_grad, vb_grad, g1_grad, b1_grad = [packed[(4 + i) * R + RF : (5 + i) * R + RF] for i in range(4)]
        return (
            block_output[None], input_grad[None], g1_grad, b1_grad,
            query_grad, key_grad, value_grad, qb_grad, vb_grad,
            output_weight_grad, ob_grad, g2_grad, b2_grad,
            up_weight_grad, ub_grad, down_weight_grad, db_grad,
        )

    return body


def solution(mesh):
    S, DP = mesh.shape["seq"], mesh.shape["dp"]
    Z = DP // 2
    parts = Mesh(mesh.devices.reshape(S, Z, 2), ("seq", "z", "core"))
    every = ("seq", "z", "core")
    token = P(("z", "core"), "seq", None)
    code = P(("z", "core"), "seq")
    vector = P(every)
    matrix = P(every, None)
    return jax.shard_map(
        make_body(S, Z),
        mesh=parts,
        in_specs=(
            token, code, code, token,
            vector, vector, matrix, matrix, matrix, vector, vector,
            matrix, vector, vector, vector, matrix, vector, matrix, vector,
        ),
        out_specs=(
            token, token, vector, vector, matrix, matrix, matrix, vector, vector,
            matrix, vector, vector, vector, matrix, vector, matrix, vector,
        ),
        check_vma=False,
    )
```

```python
import functools
import math

import jax
import jax.numpy as jnp
from jax import lax
from jax.experimental import pallas as pl
from jax.experimental.pallas import tpu as pltpu
from jax.sharding import Mesh
from jax.sharding import PartitionSpec as P

H = 16
DH = 128
EPSILON = 1e-05
NEGATIVE = -1e30
BF = jnp.bfloat16
F32 = jnp.float32
SCALE = 1.0 / math.sqrt(DH)


def dot(form, left, right):
    return jnp.einsum(form, left, right, preferred_element_type=F32)


def normalize(v):
    center = v - jnp.mean(v, axis=-1, keepdims=True)
    inv = lax.rsqrt(jnp.mean(center * center, axis=-1, keepdims=True) + EPSILON)
    return center * inv, inv


def norm_back(xhat, inv, e):
    return (
        e - jnp.mean(e, axis=-1, keepdims=True) - xhat * jnp.mean(e * xhat, axis=-1, keepdims=True)
    ) * inv


def nt(a, b):
    return lax.dot_general(a, b, (((1,), (1,)), ((), ())), preferred_element_type=F32)


def nn(a, b):
    return lax.dot_general(a, b, (((1,), (0,)), ((), ())), preferred_element_type=F32)


def tn(a, b):
    return lax.dot_general(a, b, (((0,), (0,)), ((), ())), preferred_element_type=F32)


def seen(q_ref, k_ref):
    q_pos, q_doc = q_ref[:, 0:1], q_ref[:, 1:2]
    k_pos, k_doc = k_ref[0:1, :], k_ref[1:2, :]
    return ((k_pos <= q_pos) & (k_doc == q_doc)) | (k_pos == q_pos)


def softmax(q, k, visible):
    scores = jnp.where(visible, nt(q, k) * SCALE, NEGATIVE)
    powers = jnp.exp(scores - jnp.max(scores, axis=1, keepdims=True))
    return powers / jnp.sum(powers, axis=1, keepdims=True)


def attend_kernel(heads, q_info, k_info, qkv_ref, out_ref):
    visible = seen(q_info, k_info)
    for h in range(heads):
        q, k, v = (qkv_ref[:, (part * heads + h) * DH : (part * heads + h + 1) * DH] for part in range(3))
        probs = softmax(q, k, visible).astype(BF)
        out_ref[:, h * DH : (h + 1) * DH] = nn(probs, v).astype(BF)


def attend_back_kernel(heads, q_info, k_info, qkv_ref, grad_ref, out_ref):
    visible = seen(q_info, k_info)
    for h in range(heads):
        q, k, v = (qkv_ref[:, (part * heads + h) * DH : (part * heads + h + 1) * DH] for part in range(3))
        grad = grad_ref[:, h * DH : (h + 1) * DH]
        probs = softmax(q, k, visible)
        dp = nt(grad, v)
        delta = jnp.sum(probs * dp, axis=1, keepdims=True)
        dscores = (probs * (dp - delta) * SCALE).astype(BF)
        parts = (nn(dscores, k), tn(dscores, q), tn(probs.astype(BF), grad))
        for part, value in enumerate(parts):
            out_ref[:, (part * heads + h) * DH : (part * heads + h + 1) * DH] = value.astype(BF)


def attend_call(kernel, heads, columns, matmuls, *args):
    rows = args[2].shape[0]
    return pl.pallas_call(
        functools.partial(kernel, heads),
        out_shape=jax.ShapeDtypeStruct((rows, columns), BF),
        compiler_params=pltpu.CompilerParams(vmem_limit_bytes=56 * 1024 * 1024),
        cost_estimate=pl.CostEstimate(
            flops=2 * matmuls * heads * rows * rows * DH, bytes_accessed=8 * rows * columns, transcendentals=heads * rows * rows
        ),
    )(*args)


def finish_kernel(in_ref, q_ref, k_ref, v_ref):
    places, _, wide = in_ref.shape
    cols = wide // 3
    for j in range(places):
        for part, out_ref in enumerate((q_ref, k_ref, v_ref)):
            out_ref[:, j * cols : (j + 1) * cols] = in_ref[j, :, part * cols : (part + 1) * cols].astype(F32)


def finish_qkv(v):
    places, R, wide = v.shape
    out = jax.ShapeDtypeStruct((R, places * wide // 3), F32)
    return pl.pallas_call(finish_kernel, out_shape=[out] * 3)(v)


def widen_kernel(in_ref, *refs):
    refs[-1][...] = in_ref[...].astype(F32)


def widen_first(v, columns):
    R, own = v.shape
    block = columns - own
    return pl.pallas_call(
        widen_kernel,
        grid=(own // block,),
        in_specs=[pl.BlockSpec((R, block), lambda j: (0, j))],
        out_specs=pl.BlockSpec((R, block), lambda j: (0, j)),
        out_shape=jax.ShapeDtypeStruct((R, columns), F32),
    )(v)


def widen_last(v, into):
    R, block = v.shape
    last = into.shape[1] // block - 1
    return pl.pallas_call(
        widen_kernel,
        grid=(1,),
        in_specs=[pl.BlockSpec((R, block), lambda j: (0, 0)), pl.BlockSpec(memory_space=pl.ANY)],
        out_specs=pl.BlockSpec((R, block), lambda j: (0, last)),
        out_shape=jax.ShapeDtypeStruct(into.shape, F32),
        input_output_aliases={1: 0},
    )(v, into)


def spread_kernel(starts, width, in_ref, out_ref):
    for j, row in enumerate(starts):
        for i, to in enumerate(row):
            out_ref[:, to * width : (to + 1) * width] = in_ref[j, :, i * width : (i + 1) * width].astype(F32)


def finish_up(v, S, Z):
    places, R, wide = v.shape
    width = wide // Z
    starts = [[((j // 2) * Z + i) * 2 + j % 2 for i in range(Z)] for j in range(places)]
    if width % 128:
        return v.reshape(S, 2, R, Z, width).transpose(2, 0, 3, 1, 4).reshape(R, -1).astype(F32)
    out = jax.ShapeDtypeStruct((R, places * wide), F32)
    return pl.pallas_call(functools.partial(spread_kernel, starts, width), out_shape=out)(v)


def reorder_kernel(order, in_ref, out_ref):
    width = in_ref.shape[1] // len(order)
    for to, at in enumerate(order):
        out_ref[:, to * width : (to + 1) * width] = in_ref[:, at * width : (at + 1) * width]


def lane_blocks(v, order):
    width = v.shape[1] // len(order)
    if width % 128:
        return jnp.concatenate([v[:, i * width : (i + 1) * width] for i in order], axis=1)
    return pl.pallas_call(
        functools.partial(reorder_kernel, order),
        out_shape=jax.ShapeDtypeStruct(v.shape, v.dtype),
        cost_estimate=pl.CostEstimate(flops=0, bytes_accessed=2 * v.size * v.dtype.itemsize, transcendentals=0),
    )(v)


def after(values, *others):
    return lax.optimization_barrier((values, others))[0]


def make_body(S, Z):
    every = ("seq", "z", "core")
    join = functools.partial(jnp.concatenate, axis=0)

    def flip(v, axis, size, q):
        return lax.ppermute(v, axis, [(i, i ^ q) for i in range(size)])

    def xor_seq(v, q):
        return flip(v, "seq", S, q)

    def swap_core(v):
        return flip(v, "core", 2, 1)

    def rows(v, block, t):
        return v[block * t : (block + 1) * t]

    def plane_gather(v):
        own = join([v] + [xor_seq(v, q) for q in range(1, S)])
        return own, swap_core(own)

    def plane_scatter(own, other):
        total = own + swap_core(other).astype(F32)
        t = total.shape[0] // S
        got = [xor_seq(rows(total, q, t).astype(BF), q) for q in range(1, S)]
        return rows(total, 0, t), got

    def add_up(mine, got):
        for v in got:
            mine = mine + v.astype(F32)
        return mine

    def exchange(v, axes):
        return lax.all_to_all(v, axes, split_axis=0, concat_axis=0, tiled=True)

    def spread_scatter(v, axis, size, me):
        got = [flip(lax.dynamic_index_in_dim(v, me ^ q, 0, False), axis, size, q) for q in range(1, size)]
        return add_up(lax.dynamic_index_in_dim(v, me, 0, False).astype(F32), got)

    def body(
        tokens, segment_ids, pad_mask, cotangent,
        first_gain, first_shift, query_weight, key_weight, value_weight, query_bias, value_bias,
        output_weight, output_bias, second_gain, second_shift, up_weight, up_bias, down_weight, down_bias,
    ):
        s, z, c = (lax.axis_index(a) for a in every)
        n, tp = S * Z * 2, S * 2
        R, D = query_weight.shape
        RF = down_weight.shape[0]
        t = tokens.shape[1]
        L = S * t
        heads_own = H // tp
        cols = D // tp
        half = Z // 2
        both = range(2)

        natural = [i_s * Z + i_z for i_z in range(Z) for i_s in range(S)]
        back = [natural.index(i) for i in range(S * Z)]

        pieces = [w.reshape(R, tp, cols).transpose(1, 0, 2) for w in (query_weight, key_weight, value_weight)]
        up = up_weight.reshape(R, S, Z, 2, RF).transpose(1, 3, 0, 2, 4).reshape(tp, R, Z * RF)
        qkv = exchange(jnp.concatenate(pieces, axis=2), ("seq", "core")).reshape(tp * R, 3 * cols)
        small = jnp.concatenate(
            [first_gain, first_shift, query_bias, value_bias, output_bias, second_gain, second_shift, down_bias, up_bias]
        )
        small = exchange(jnp.broadcast_to(after(small, qkv)[None], (n, small.shape[0])), every)
        small_there = small
        small = small.astype(F32)
        g1, b1, qb, vb, ob, g2, b2, db = [small[:, i * R : (i + 1) * R].reshape(-1) for i in range(8)]
        ub = small[:, 8 * R :].reshape(S, Z, 2, RF)

        wo = lax.all_gather(output_weight, "z", axis=0)
        wqkv = lax.all_gather(after(qkv, wo), "z", axis=0, tiled=True)
        up = exchange(after(up, small_there), ("seq", "core")).reshape(tp * R, Z * RF)
        wqkv, up = after((wqkv, up))
        wup = lax.all_gather(up, "z", axis=0, tiled=True)
        wdown = lax.all_gather(after(down_weight, wup), "z", axis=0, tiled=True)
        keep_part = lax.dynamic_slice_in_dim(wo, c * half, half, axis=0)
        got_part = swap_core(lax.dynamic_slice_in_dim(wo, (1 - c) * half, half, axis=0))
        wo = jnp.where(
            c == 0,
            jnp.stack([keep_part, got_part], axis=1),
            jnp.stack([got_part, keep_part], axis=1),
        ).reshape(cols, D)

        codes = jnp.stack([segment_ids[0], pad_mask[0]])
        codes = jnp.stack([codes] + [xor_seq(codes, q) for q in range(1, S)], axis=1)
        codes = [codes.reshape(2, L), swap_core(codes).reshape(2, L)]
        position = ((s ^ jnp.arange(S, dtype=jnp.int32))[:, None] * t + jnp.arange(t, dtype=jnp.int32)[None]).reshape(L)
        q_info = [jnp.stack([position, code[0]], axis=1) for code in codes]
        k_info = [jnp.stack([position, jnp.where(code[1] == 1, code[0], -1)]) for code in codes]
        keep = pad_mask[0].astype(F32)[:, None]

        xf = tokens[0].astype(F32)
        dy = cotangent[0]
        dyf = dy.astype(F32)
        xhat1, inv1 = normalize(xf)
        normed = plane_gather(lane_blocks((xhat1 * g1 + b1).astype(BF), natural))
        qkv_bias = jnp.stack([qb.reshape(tp, cols), jnp.zeros((tp, cols), F32), vb.reshape(tp, cols)], axis=1)
        qkv_bias = lax.dynamic_index_in_dim(qkv_bias, s * 2 + c, 0, keepdims=False).reshape(3 * cols)
        qkv_out, heads = [None, None], [None, None]
        for e in (1, 0):
            qkv_out[e] = (dot("td,de->te", normed[e], wqkv) + qkv_bias).astype(BF)
            heads[e] = attend_call(attend_kernel, heads_own, cols, 2, q_info[e], k_info[e], qkv_out[e])
        branch = add_up(*plane_scatter(dot("td,de->te", heads[0], wo), dot("td,de->te", heads[1], wo).astype(BF)))
        branch = after(branch, wup)
        middle = xf + (branch + ob) * keep
        xhat2, inv2 = normalize(middle)
        second = plane_gather(lane_blocks((xhat2 * g2 + b2).astype(BF), natural))
        dy_all = plane_gather(after(dy, second[0]))
        up_row = lax.dynamic_index_in_dim(lax.dynamic_index_in_dim(ub, s, 0, False), c, 1, False).reshape(Z * RF)
        active, slope = [None, None], [None, None]
        for e in both:
            hidden = dot("td,df->tf", second[e], wup) + up_row
            phi = 0.5 * (1.0 + lax.erf(hidden * math.sqrt(0.5)))
            slope[e] = phi + hidden * jnp.exp(-0.5 * hidden * hidden) * (1.0 / math.sqrt(2 * math.pi))
            active[e] = (hidden * phi).astype(BF)
        early = D - D // 4
        active_join, dy_join = join(active), join(dy_all)
        down_grad = dot("tf,td->fd", active_join, dy_join[:, :early]).astype(BF)
        down_grad, wdown = after((down_grad, wdown))
        down_early = lax.psum_scatter(down_grad, "z", scatter_dimension=0, tiled=True)
        dhidden = [None, None]
        for e in (1, 0):
            dhidden[e] = (dot("td,fd->tf", dy_all[e], wdown) * slope[e]).astype(BF)

        mine, got = plane_scatter(
            dot("tf,df->td", dhidden[0], wup), dot("tf,df->td", dhidden[1], wup).astype(BF)
        )
        fill_dhidden, fill_second = after((dhidden, second), got)
        dhidden_join = join(fill_dhidden)
        up_grad = dot("td,tf->df", join(fill_second), dhidden_join).astype(BF)
        up_mm = up_grad
        active_join, dy_join = after((active_join, dy_join), up_mm)
        down_rest = dot("tf,td->fd", active_join, dy_join[:, early:]).astype(BF)
        up_grad = lax.psum_scatter(after(up_grad, down_early), "z", scatter_dimension=0, tiled=True)
        dsecond = lane_blocks(add_up(mine, got), back)
        dsecond = after(dsecond, down_early, up_mm, down_rest)
        dmiddle = dyf + norm_back(xhat2, inv2, g2 * dsecond)
        dbranch = (dmiddle * keep).astype(BF)
        dbranch_all = plane_gather(dbranch)
        active = after(active, dbranch)
        result = dot("tf,fd->td", active[0], wdown) + swap_core(dot("tf,fd->td", active[1], wdown).astype(BF)).astype(F32)
        wo_grad = dot("td,te->de", heads[0], dbranch_all[0]) + dot("td,te->de", heads[1], dbranch_all[1])
        wo_grad = wo_grad.astype(BF).reshape(half, 2, R, D)
        keep_part = lax.dynamic_index_in_dim(wo_grad, c, 1, False)
        got_part = swap_core(lax.dynamic_index_in_dim(wo_grad, 1 - c, 1, False))
        result, dbranch_all = after((result, dbranch_all))
        result_got = [xor_seq(rows(result, q, t).astype(BF), q) for q in range(1, S)]
        dqkv = [None, None]
        for e in both:
            dheads = dot("te,de->td", dbranch_all[e], wo).astype(BF)
            dqkv[e] = attend_call(attend_back_kernel, heads_own, 3 * cols, 5, q_info[e], k_info[e], qkv_out[e], dheads)
        qkv_grad = (dot("td,te->de", normed[0], dqkv[0]) + dot("td,te->de", normed[1], dqkv[1])).astype(BF)
        wo_grad = jnp.where(c == 0, join([keep_part, got_part]), join([got_part, keep_part]))
        result = add_up(rows(result, 0, t), after(result_got, qkv_grad))
        mixed = jnp.concatenate([qkv_grad, wo_grad.reshape(D, -1)], axis=1)
        dqkv = after(dqkv, mixed)
        mixed = lax.psum_scatter(after(mixed, up_grad, result_got), "z", scatter_dimension=0, tiled=True)
        mixed_sum = mixed
        qkv_grad = exchange(mixed[:, : 3 * cols].reshape(tp, R, 3 * cols), ("seq", "core"))
        output_weight_grad = mixed[:, 3 * cols :].reshape(R, D).astype(F32)
        mine, got = plane_scatter(dot("te,de->td", dqkv[0], wqkv), dot("te,de->td", dqkv[1], wqkv).astype(BF))
        up_grad = exchange(up_grad.reshape(tp, R, Z * RF), ("seq", "core"))
        mine, got = after((mine, got), up_grad)
        dnormed = lane_blocks(add_up(mine, got), back)
        input_grad = dmiddle + norm_back(xhat1, inv1, g1 * dnormed)
        block_output = (middle + result + db).astype(BF)
        up_grad = after(up_grad, mixed_sum)
        up_weight_grad = finish_up(up_grad.reshape(tp, R, Z * RF), S, Z)
        down_rest = lax.psum_scatter(after(down_rest, mixed_sum), "z", scatter_dimension=0, tiled=True)
        down_weight_grad = widen_last(down_rest, widen_first(down_early, D))
        query_grad, key_grad, value_grad = finish_qkv(qkv_grad)

        bias = sum(jnp.sum(v.astype(F32), axis=0) for v in dqkv).reshape(3, cols)
        spread = jnp.zeros((2, tp, cols), F32)
        spread = lax.dynamic_update_slice(spread, jnp.stack([bias[0], bias[2]])[:, None], (0, s * 2 + c, 0))
        wide = jnp.zeros((S, Z, 2, RF), F32)
        wide = lax.dynamic_update_slice(
            wide, jnp.sum(dhidden_join.astype(F32), axis=0).reshape(1, Z, 1, RF), (s, 0, c, 0)
        )
        vectors = [
            jnp.sum(dbranch.astype(F32), axis=0),
            jnp.sum(dsecond * xhat2, axis=0),
            jnp.sum(dsecond, axis=0),
            jnp.sum(dyf, axis=0),
            wide,
            spread[0],
            spread[1],
            jnp.sum(dnormed * xhat1, axis=0),
            jnp.sum(dnormed, axis=0),
        ]
        packed = jnp.concatenate([v.reshape(S, Z, 2, -1) for v in vectors], axis=3)
        packed = lax.dynamic_index_in_dim(packed, c, 2, False) + swap_core(lax.dynamic_index_in_dim(packed, 1 - c, 2, False))
        packed = spread_scatter(packed, "seq", S, s)
        packed = spread_scatter(after(packed, qkv_grad, up_weight_grad, output_weight_grad), "z", Z, z)
        ob_grad, g2_grad, b2_grad, db_grad = [packed[i * R : (i + 1) * R] for i in range(4)]
        ub_grad = packed[4 * R : 4 * R + RF]
        qb_grad, vb_grad, g1_grad, b1_grad = [packed[(4 + i) * R + RF : (5 + i) * R + RF] for i in range(4)]
        return (
            block_output[None], input_grad[None], g1_grad, b1_grad,
            query_grad, key_grad, value_grad, qb_grad, vb_grad,
            output_weight_grad, ob_grad, g2_grad, b2_grad,
            up_weight_grad, ub_grad, down_weight_grad, db_grad,
        )

    return body


def solution(mesh):
    S, DP = mesh.shape["seq"], mesh.shape["dp"]
    Z = DP // 2
    parts = Mesh(mesh.devices.reshape(S, Z, 2), ("seq", "z", "core"))
    every = ("seq", "z", "core")
    token = P(("z", "core"), "seq", None)
    code = P(("z", "core"), "seq")
    vector = P(every)
    matrix = P(every, None)
    return jax.shard_map(
        make_body(S, Z),
        mesh=parts,
        in_specs=(
            token, code, code, token,
            vector, vector, matrix, matrix, matrix, vector, vector,
            matrix, vector, vector, vector, matrix, vector, matrix, vector,
        ),
        out_specs=(
            token, token, vector, vector, matrix, matrix, matrix, vector, vector,
            matrix, vector, vector, vector, matrix, vector, matrix, vector,
        ),
        check_vma=False,
    )
```

```python
import functools
import math

import jax
import jax.numpy as jnp
from jax import lax
from jax.experimental import pallas as pl
from jax.experimental.pallas import tpu as pltpu
from jax.sharding import Mesh
from jax.sharding import PartitionSpec as P

H = 16
DH = 128
EPSILON = 1e-05
NEGATIVE = -1e30
BF = jnp.bfloat16
F32 = jnp.float32
SCALE = 1.0 / math.sqrt(DH)


def dot(form, left, right):
    return jnp.einsum(form, left, right, preferred_element_type=F32)


def normalize(v):
    center = v - jnp.mean(v, axis=-1, keepdims=True)
    inv = lax.rsqrt(jnp.mean(center * center, axis=-1, keepdims=True) + EPSILON)
    return center * inv, inv


def norm_back(xhat, inv, e):
    return (
        e - jnp.mean(e, axis=-1, keepdims=True) - xhat * jnp.mean(e * xhat, axis=-1, keepdims=True)
    ) * inv


def nt(a, b):
    return lax.dot_general(a, b, (((1,), (1,)), ((), ())), preferred_element_type=F32)


def nn(a, b):
    return lax.dot_general(a, b, (((1,), (0,)), ((), ())), preferred_element_type=F32)


def tn(a, b):
    return lax.dot_general(a, b, (((0,), (0,)), ((), ())), preferred_element_type=F32)


def seen(q_ref, k_ref):
    q_pos, q_doc = q_ref[:, 0:1], q_ref[:, 1:2]
    k_pos, k_doc = k_ref[0:1, :], k_ref[1:2, :]
    return ((k_pos <= q_pos) & (k_doc == q_doc)) | (k_pos == q_pos)


def softmax(q, k, visible):
    scores = jnp.where(visible, nt(q, k) * SCALE, NEGATIVE)
    powers = jnp.exp(scores - jnp.max(scores, axis=1, keepdims=True))
    return powers / jnp.sum(powers, axis=1, keepdims=True)


def attend_kernel(heads, q_info, k_info, qkv_ref, out_ref):
    visible = seen(q_info, k_info)
    for h in range(heads):
        q, k, v = (qkv_ref[:, (part * heads + h) * DH : (part * heads + h + 1) * DH] for part in range(3))
        probs = softmax(q, k, visible).astype(BF)
        out_ref[:, h * DH : (h + 1) * DH] = nn(probs, v).astype(BF)


def attend_back_kernel(heads, q_info, k_info, qkv_ref, grad_ref, out_ref):
    visible = seen(q_info, k_info)
    for h in range(heads):
        q, k, v = (qkv_ref[:, (part * heads + h) * DH : (part * heads + h + 1) * DH] for part in range(3))
        grad = grad_ref[:, h * DH : (h + 1) * DH]
        probs = softmax(q, k, visible)
        dp = nt(grad, v)
        delta = jnp.sum(probs * dp, axis=1, keepdims=True)
        dscores = (probs * (dp - delta) * SCALE).astype(BF)
        parts = (nn(dscores, k), tn(dscores, q), tn(probs.astype(BF), grad))
        for part, value in enumerate(parts):
            out_ref[:, (part * heads + h) * DH : (part * heads + h + 1) * DH] = value.astype(BF)


def attend_call(kernel, heads, columns, matmuls, *args):
    rows = args[2].shape[0]
    return pl.pallas_call(
        functools.partial(kernel, heads),
        out_shape=jax.ShapeDtypeStruct((rows, columns), BF),
        compiler_params=pltpu.CompilerParams(vmem_limit_bytes=56 * 1024 * 1024),
        cost_estimate=pl.CostEstimate(
            flops=2 * matmuls * heads * rows * rows * DH, bytes_accessed=8 * rows * columns, transcendentals=heads * rows * rows
        ),
    )(*args)


def finish_kernel(in_ref, q_ref, k_ref, v_ref):
    places, _, wide = in_ref.shape
    cols = wide // 3
    for j in range(places):
        for part, out_ref in enumerate((q_ref, k_ref, v_ref)):
            out_ref[:, j * cols : (j + 1) * cols] = in_ref[j, :, part * cols : (part + 1) * cols].astype(F32)


def finish_qkv(v):
    places, R, wide = v.shape
    out = jax.ShapeDtypeStruct((R, places * wide // 3), F32)
    return pl.pallas_call(finish_kernel, out_shape=[out] * 3)(v)


def widen_kernel(in_ref, *refs):
    refs[-1][...] = in_ref[...].astype(F32)


def widen_first(v, columns):
    R, own = v.shape
    block = columns - own
    return pl.pallas_call(
        widen_kernel,
        grid=(own // block,),
        in_specs=[pl.BlockSpec((R, block), lambda j: (0, j))],
        out_specs=pl.BlockSpec((R, block), lambda j: (0, j)),
        out_shape=jax.ShapeDtypeStruct((R, columns), F32),
    )(v)


def widen_last(v, into):
    R, block = v.shape
    last = into.shape[1] // block - 1
    return pl.pallas_call(
        widen_kernel,
        grid=(1,),
        in_specs=[pl.BlockSpec((R, block), lambda j: (0, 0)), pl.BlockSpec(memory_space=pl.ANY)],
        out_specs=pl.BlockSpec((R, block), lambda j: (0, last)),
        out_shape=jax.ShapeDtypeStruct(into.shape, F32),
        input_output_aliases={1: 0},
    )(v, into)


def spread_kernel(starts, width, in_ref, out_ref):
    for j, row in enumerate(starts):
        for i, to in enumerate(row):
            out_ref[:, to * width : (to + 1) * width] = in_ref[j, :, i * width : (i + 1) * width].astype(F32)


def finish_up(v, S, Z):
    places, R, wide = v.shape
    width = wide // Z
    starts = [[((j // 2) * Z + i) * 2 + j % 2 for i in range(Z)] for j in range(places)]
    if width % 128:
        return v.reshape(S, 2, R, Z, width).transpose(2, 0, 3, 1, 4).reshape(R, -1).astype(F32)
    out = jax.ShapeDtypeStruct((R, places * wide), F32)
    return pl.pallas_call(functools.partial(spread_kernel, starts, width), out_shape=out)(v)


def reorder_kernel(order, in_ref, out_ref):
    width = in_ref.shape[1] // len(order)
    for to, at in enumerate(order):
        out_ref[:, to * width : (to + 1) * width] = in_ref[:, at * width : (at + 1) * width]


def lane_blocks(v, order):
    width = v.shape[1] // len(order)
    if width % 128:
        return jnp.concatenate([v[:, i * width : (i + 1) * width] for i in order], axis=1)
    return pl.pallas_call(
        functools.partial(reorder_kernel, order),
        out_shape=jax.ShapeDtypeStruct(v.shape, v.dtype),
        cost_estimate=pl.CostEstimate(flops=0, bytes_accessed=2 * v.size * v.dtype.itemsize, transcendentals=0),
    )(v)


def after(values, *others):
    return lax.optimization_barrier((values, others))[0]


def make_body(S, Z):
    every = ("seq", "z", "core")
    join = functools.partial(jnp.concatenate, axis=0)

    def flip(v, axis, size, q):
        return lax.ppermute(v, axis, [(i, i ^ q) for i in range(size)])

    def xor_seq(v, q):
        return flip(v, "seq", S, q)

    def swap_core(v):
        return flip(v, "core", 2, 1)

    def rows(v, block, t):
        return v[block * t : (block + 1) * t]

    def plane_gather(v):
        own = join([v] + [xor_seq(v, q) for q in range(1, S)])
        return own, swap_core(own)

    def plane_scatter(own, other):
        total = own + swap_core(other).astype(F32)
        t = total.shape[0] // S
        got = [xor_seq(rows(total, q, t).astype(BF), q) for q in range(1, S)]
        return rows(total, 0, t), got

    def add_up(mine, got):
        for v in got:
            mine = mine + v.astype(F32)
        return mine

    def exchange(v, axes):
        return lax.all_to_all(v, axes, split_axis=0, concat_axis=0, tiled=True)

    def spread_scatter(v, axis, size, me):
        got = [flip(lax.dynamic_index_in_dim(v, me ^ q, 0, False), axis, size, q) for q in range(1, size)]
        return add_up(lax.dynamic_index_in_dim(v, me, 0, False).astype(F32), got)

    def body(
        tokens, segment_ids, pad_mask, cotangent,
        first_gain, first_shift, query_weight, key_weight, value_weight, query_bias, value_bias,
        output_weight, output_bias, second_gain, second_shift, up_weight, up_bias, down_weight, down_bias,
    ):
        s, z, c = (lax.axis_index(a) for a in every)
        n, tp = S * Z * 2, S * 2
        R, D = query_weight.shape
        RF = down_weight.shape[0]
        t = tokens.shape[1]
        L = S * t
        heads_own = H // tp
        cols = D // tp
        half = Z // 2
        both = range(2)

        natural = [i_s * Z + i_z for i_z in range(Z) for i_s in range(S)]
        back = [natural.index(i) for i in range(S * Z)]

        pieces = [w.reshape(R, tp, cols).transpose(1, 0, 2) for w in (query_weight, key_weight, value_weight)]
        up = up_weight.reshape(R, S, Z, 2, RF).transpose(1, 3, 0, 2, 4).reshape(tp, R, Z * RF)
        qkv = exchange(jnp.concatenate(pieces, axis=2), ("seq", "core")).reshape(tp * R, 3 * cols)
        small = jnp.concatenate(
            [first_gain, first_shift, query_bias, value_bias, output_bias, second_gain, second_shift, down_bias, up_bias]
        )
        small = exchange(jnp.broadcast_to(after(small, qkv)[None], (n, small.shape[0])), every)
        small_there = small
        small = small.astype(F32)
        g1, b1, qb, vb, ob, g2, b2, db = [small[:, i * R : (i + 1) * R].reshape(-1) for i in range(8)]
        ub = small[:, 8 * R :].reshape(S, Z, 2, RF)

        wo = lax.all_gather(output_weight, "z", axis=0)
        wqkv = lax.all_gather(after(qkv, wo), "z", axis=0, tiled=True)
        up = exchange(after(up, small_there), ("seq", "core")).reshape(tp * R, Z * RF)
        wqkv, up = after((wqkv, up))
        wup = lax.all_gather(up, "z", axis=0, tiled=True)
        wdown = lax.all_gather(after(down_weight, wup), "z", axis=0, tiled=True)
        keep_part = lax.dynamic_slice_in_dim(wo, c * half, half, axis=0)
        got_part = swap_core(lax.dynamic_slice_in_dim(wo, (1 - c) * half, half, axis=0))
        wo = jnp.where(
            c == 0,
            jnp.stack([keep_part, got_part], axis=1),
            jnp.stack([got_part, keep_part], axis=1),
        ).reshape(cols, D)

        codes = jnp.stack([segment_ids[0], pad_mask[0]])
        codes = jnp.stack([codes] + [xor_seq(codes, q) for q in range(1, S)], axis=1)
        codes = [codes.reshape(2, L), swap_core(codes).reshape(2, L)]
        position = ((s ^ jnp.arange(S, dtype=jnp.int32))[:, None] * t + jnp.arange(t, dtype=jnp.int32)[None]).reshape(L)
        q_info = [jnp.stack([position, code[0]], axis=1) for code in codes]
        k_info = [jnp.stack([position, jnp.where(code[1] == 1, code[0], -1)]) for code in codes]
        keep = pad_mask[0].astype(F32)[:, None]

        xf = tokens[0].astype(F32)
        dy = cotangent[0]
        dyf = dy.astype(F32)
        xhat1, inv1 = normalize(xf)
        normed = plane_gather(lane_blocks((xhat1 * g1 + b1).astype(BF), natural))
        qkv_bias = jnp.stack([qb.reshape(tp, cols), jnp.zeros((tp, cols), F32), vb.reshape(tp, cols)], axis=1)
        qkv_bias = lax.dynamic_index_in_dim(qkv_bias, s * 2 + c, 0, keepdims=False).reshape(3 * cols)
        qkv_out, heads = [None, None], [None, None]
        for e in (1, 0):
            qkv_out[e] = (dot("td,de->te", normed[e], wqkv) + qkv_bias).astype(BF)
            heads[e] = attend_call(attend_kernel, heads_own, cols, 2, q_info[e], k_info[e], qkv_out[e])
        branch = add_up(*plane_scatter(dot("td,de->te", heads[0], wo), dot("td,de->te", heads[1], wo).astype(BF)))
        branch = after(branch, wup)
        middle = xf + (branch + ob) * keep
        xhat2, inv2 = normalize(middle)
        second = plane_gather(lane_blocks((xhat2 * g2 + b2).astype(BF), natural))
        dy_all = plane_gather(after(dy, second[0]))
        up_row = lax.dynamic_index_in_dim(lax.dynamic_index_in_dim(ub, s, 0, False), c, 1, False).reshape(Z * RF)
        active, slope = [None, None], [None, None]
        for e in both:
            hidden = dot("td,df->tf", second[e], wup) + up_row
            phi = 0.5 * (1.0 + lax.erf(hidden * math.sqrt(0.5)))
            slope[e] = phi + hidden * jnp.exp(-0.5 * hidden * hidden) * (1.0 / math.sqrt(2 * math.pi))
            active[e] = (hidden * phi).astype(BF)
        early = D - D // 4
        active_join, dy_join = join(active), join(dy_all)
        down_grad = dot("tf,td->fd", active_join, dy_join[:, :early]).astype(BF)
        down_grad, wdown = after((down_grad, wdown))
        down_early = lax.psum_scatter(down_grad, "z", scatter_dimension=0, tiled=True)
        dhidden = [None, None]
        for e in (1, 0):
            dhidden[e] = (dot("td,fd->tf", dy_all[e], wdown) * slope[e]).astype(BF)

        mine, got = plane_scatter(
            dot("tf,df->td", dhidden[0], wup), dot("tf,df->td", dhidden[1], wup).astype(BF)
        )
        fill_dhidden, fill_second = after((dhidden, second), got)
        dhidden_join = join(fill_dhidden)
        up_grad = dot("td,tf->df", join(fill_second), dhidden_join).astype(BF)
        up_mm = up_grad
        up_grad = lax.psum_scatter(after(up_grad, down_early), "z", scatter_dimension=0, tiled=True)
        dsecond = lane_blocks(add_up(mine, got), back)
        dsecond = after(dsecond, down_early, up_mm)
        dmiddle = dyf + norm_back(xhat2, inv2, g2 * dsecond)
        dbranch = (dmiddle * keep).astype(BF)
        dbranch_all = plane_gather(dbranch)
        active = after(active, dbranch)
        result = dot("tf,fd->td", active[0], wdown) + swap_core(dot("tf,fd->td", active[1], wdown).astype(BF)).astype(F32)
        wo_grad = dot("td,te->de", heads[0], dbranch_all[0]) + dot("td,te->de", heads[1], dbranch_all[1])
        wo_grad = wo_grad.astype(BF).reshape(half, 2, R, D)
        keep_part = lax.dynamic_index_in_dim(wo_grad, c, 1, False)
        got_part = swap_core(lax.dynamic_index_in_dim(wo_grad, 1 - c, 1, False))
        result, dbranch_all = after((result, dbranch_all))
        result_got = [xor_seq(rows(result, q, t).astype(BF), q) for q in range(1, S)]
        dqkv = [None, None]
        for e in both:
            dheads = dot("te,de->td", dbranch_all[e], wo).astype(BF)
            dqkv[e] = attend_call(attend_back_kernel, heads_own, 3 * cols, 5, q_info[e], k_info[e], qkv_out[e], dheads)
        qkv_grad = (dot("td,te->de", normed[0], dqkv[0]) + dot("td,te->de", normed[1], dqkv[1])).astype(BF)
        wo_grad = jnp.where(c == 0, join([keep_part, got_part]), join([got_part, keep_part]))
        result = add_up(rows(result, 0, t), after(result_got, qkv_grad))
        mixed = jnp.concatenate([qkv_grad, wo_grad.reshape(D, -1)], axis=1)
        dqkv = after(dqkv, mixed)
        active_join, dy_join = after((active_join, dy_join), mixed)
        down_rest = dot("tf,td->fd", active_join, dy_join[:, early:]).astype(BF)
        mixed = lax.psum_scatter(after(mixed, up_grad, result_got), "z", scatter_dimension=0, tiled=True)
        mixed_sum = mixed
        qkv_grad = exchange(mixed[:, : 3 * cols].reshape(tp, R, 3 * cols), ("seq", "core"))
        output_weight_grad = mixed[:, 3 * cols :].reshape(R, D).astype(F32)
        mine, got = plane_scatter(dot("te,de->td", dqkv[0], wqkv), dot("te,de->td", dqkv[1], wqkv).astype(BF))
        up_grad = exchange(up_grad.reshape(tp, R, Z * RF), ("seq", "core"))
        mine, got = after((mine, got), up_grad)
        dnormed = lane_blocks(add_up(mine, got), back)
        input_grad = dmiddle + norm_back(xhat1, inv1, g1 * dnormed)
        block_output = (middle + result + db).astype(BF)
        up_grad = after(up_grad, mixed_sum)
        up_weight_grad = finish_up(up_grad.reshape(tp, R, Z * RF), S, Z)
        down_rest = lax.psum_scatter(after(down_rest, mixed_sum), "z", scatter_dimension=0, tiled=True)
        down_weight_grad = widen_last(down_rest, widen_first(down_early, D))
        query_grad, key_grad, value_grad = finish_qkv(qkv_grad)

        bias = sum(jnp.sum(v.astype(F32), axis=0) for v in dqkv).reshape(3, cols)
        spread = jnp.zeros((2, tp, cols), F32)
        spread = lax.dynamic_update_slice(spread, jnp.stack([bias[0], bias[2]])[:, None], (0, s * 2 + c, 0))
        wide = jnp.zeros((S, Z, 2, RF), F32)
        wide = lax.dynamic_update_slice(
            wide, jnp.sum(dhidden_join.astype(F32), axis=0).reshape(1, Z, 1, RF), (s, 0, c, 0)
        )
        vectors = [
            jnp.sum(dbranch.astype(F32), axis=0),
            jnp.sum(dsecond * xhat2, axis=0),
            jnp.sum(dsecond, axis=0),
            jnp.sum(dyf, axis=0),
            wide,
            spread[0],
            spread[1],
            jnp.sum(dnormed * xhat1, axis=0),
            jnp.sum(dnormed, axis=0),
        ]
        packed = jnp.concatenate([v.reshape(S, Z, 2, -1) for v in vectors], axis=3)
        packed = lax.dynamic_index_in_dim(packed, c, 2, False) + swap_core(lax.dynamic_index_in_dim(packed, 1 - c, 2, False))
        packed = spread_scatter(packed, "seq", S, s)
        packed = spread_scatter(after(packed, qkv_grad, up_weight_grad, output_weight_grad), "z", Z, z)
        ob_grad, g2_grad, b2_grad, db_grad = [packed[i * R : (i + 1) * R] for i in range(4)]
        ub_grad = packed[4 * R : 4 * R + RF]
        qb_grad, vb_grad, g1_grad, b1_grad = [packed[(4 + i) * R + RF : (5 + i) * R + RF] for i in range(4)]
        return (
            block_output[None], input_grad[None], g1_grad, b1_grad,
            query_grad, key_grad, value_grad, qb_grad, vb_grad,
            output_weight_grad, ob_grad, g2_grad, b2_grad,
            up_weight_grad, ub_grad, down_weight_grad, db_grad,
        )

    return body


def solution(mesh):
    S, DP = mesh.shape["seq"], mesh.shape["dp"]
    Z = DP // 2
    parts = Mesh(mesh.devices.reshape(S, Z, 2), ("seq", "z", "core"))
    every = ("seq", "z", "core")
    token = P(("z", "core"), "seq", None)
    code = P(("z", "core"), "seq")
    vector = P(every)
    matrix = P(every, None)
    return jax.shard_map(
        make_body(S, Z),
        mesh=parts,
        in_specs=(
            token, code, code, token,
            vector, vector, matrix, matrix, matrix, vector, vector,
            matrix, vector, vector, vector, matrix, vector, matrix, vector,
        ),
        out_specs=(
            token, token, vector, vector, matrix, matrix, matrix, vector, vector,
            matrix, vector, vector, vector, matrix, vector, matrix, vector,
        ),
        check_vma=False,
    )
```
